512 devices in a mesh: dom: 16 (over z_lo, y), ch: 32 (over z_hi, x, core).
Axes of the slice: x: 4, y: 4, z: 16 (z_hi: 4, z_lo: 4; z = z_hi * 4 + z_lo), core: 2. Of those that a mesh axis runs over, the one named last changes fastest.
Arguments:
- node_feats: bfloat16 [262144, 128], P(('dom', 'ch')), may hold values from -6 to 6
- positions: bfloat16 [3, 262144], P(None, ('dom', 'ch'))
- species: int32 [262144], P(('dom', 'ch')), may hold values from 0 to 88
- neighbours: int32 [262144, 32], P(('dom', 'ch')), may hold values from 0 to 767
- counts: int32 [262144], P(('dom', 'ch')), may hold values from 8 to 32
- ghost_ids: int32 [2, 32768], P(None, ('dom', 'ch')), may hold values from 0 to 511, as said below
- w_node: bfloat16 [128, 128], replicated, may hold values from -0.5 to 0.5
- w_r1: bfloat16 [8, 64], replicated, may hold values from -3 to 3
- w_r2: bfloat16 [64, 64], replicated, may hold values from -1 to 1
- w_r3: bfloat16 [64, 64], replicated, may hold values from -1 to 1
- w_r4: bfloat16 [64, 512], replicated, may hold values from -1 to 1
- w_out: bfloat16 [512, 128], replicated, may hold values from -0.5 to 0.5
- species_emb: bfloat16 [89, 128], replicated, may hold values from -3 to 3
Outputs:
- updated: bfloat16 [262144, 128], P(('dom', 'ch'))
The draws below stay inside these ranges and needn't reach their ends.
Inputs may be any that keep to these rules, and one draw needn't show every extreme that they name: `ghost_ids`: the entries of both rows that belong to one block are all distinct.
All inputs are finite; a program needn't handle non-finite values.
Results may differ from the reference program's by a relative error of at most 0.0084.
Values may be sent and summed in bfloat16 or wider, within the bound.
A program may use at most 64 MiB of HBM per device.

```python
import math
import jax
import jax.numpy as jnp
from jax import lax

C = 128
S = 89
HID = 64
NB = 8
K = 32
A_DEV = 512
G_DEV = 64
DOM_ATOMS = 16384
LOC = 768
ATOMS = 262144
N_DOM = 16
N_CH = 32


def shuffle(one_key):
    return jax.random.permutation(one_key, A_DEV)


def ghost_layout(key):
    blocks_all = ATOMS // A_DEV
    key_list = jax.random.split(jax.random.fold_in(key, 101), blocks_all)
    orders = jax.vmap(shuffle)(key_list).astype(jnp.int32)
    to_lower = orders[:, :G_DEV]
    to_upper = orders[:, G_DEV:2 * G_DEV]
    middle = jax.random.randint(jax.random.fold_in(key, 102), (blocks_all, A_DEV), 1, 3, dtype=jnp.int32)
    row_index = jnp.arange(blocks_all, dtype=jnp.int32)[:, None]
    cell_index = middle.at[row_index, to_lower].set(0).at[row_index, to_upper].set(3)
    return (to_lower, to_upper, cell_index)


def draw_ghost_ids(key, part):
    to_lower, to_upper, cell_index = ghost_layout(key)
    return jnp.stack([to_lower.reshape(-1), to_upper.reshape(-1)]).astype(jnp.int32)


def draw_positions(key, part):
    to_lower, to_upper, cell_index = ghost_layout(key)
    key = jax.random.fold_in(key, 5)
    first_key, second_key, third_key = jax.random.split(key, 3)
    first = cell_index.reshape(-1).astype(jnp.float32) + jax.random.uniform(first_key, (ATOMS,), jnp.float32)
    place = (jnp.arange(ATOMS, dtype=jnp.int32) % DOM_ATOMS).astype(jnp.float32)
    second = 4.0 * (place + jax.random.uniform(second_key, (ATOMS,), jnp.float32)) / DOM_ATOMS
    third = jax.random.uniform(third_key, (ATOMS,), jnp.float32, 0.0, 4.0)
    return jnp.stack([first, second, third]).astype(jnp.bfloat16)


def draw_neighbours(key, part):
    to_lower, to_upper, cell_index = ghost_layout(key)
    key = jax.random.fold_in(key, 7)
    offset_key, pick_key, ghost_key = jax.random.split(key, 3)
    cells = cell_index.reshape(ATOMS)[:, None]
    place = (jnp.arange(ATOMS, dtype=jnp.int32) % A_DEV)[:, None]
    offset = jax.random.randint(offset_key, (ATOMS, K), -G_DEV, G_DEV + 1, dtype=jnp.int32)
    window = G_DEV + place + offset
    picked = jax.random.randint(pick_key, (ATOMS, K), 0, 4, dtype=jnp.int32)
    slot_index = jnp.arange(K, dtype=jnp.int32)[None, :]
    facing = (cells == 0) | (cells == 3)
    use_ghost = facing & ((slot_index == 0) | (picked == 0))
    ghost_row = A_DEV + 2 * G_DEV + jnp.where(cells == 3, G_DEV, 0) + jax.random.randint(ghost_key, (ATOMS, K), 0, G_DEV, dtype=jnp.int32)
    return jnp.where(use_ghost, ghost_row, window).astype(jnp.int32)


def with_ends(entries, rng, smallest, high):
    longest = entries.shape.index(max(entries.shape))
    spots = []
    for shift in (0, 1):
        where = [jax.random.randint(jax.random.fold_in(rng, axis), (), 0, length) for axis, length in enumerate(entries.shape)]
        where[longest] = (where[longest] + shift) % entries.shape[longest]
        spots.append(tuple(where))
    return entries.at[spots[0]].set(smallest).at[spots[1]].set(high)


def level_of(key, extent, cuts, smallest, high):
    loudness, own = 1.0, jax.random.fold_in(key, 6)
    for position, blocks in cuts:
        steps = jnp.exp(jax.random.uniform(jax.random.fold_in(own, position), (blocks,), jnp.float32, smallest / len(cuts), high / len(cuts)))
        loudness = loudness * jnp.repeat(steps, extent[position] // blocks).reshape([-1 if axis == position else 1 for axis in range(len(extent))])
    return loudness


def bell_draw(rng, shape, scale, limit, cuts=(), kind=jnp.bfloat16):
    loudness = level_of(rng, shape, cuts, -0.22, 0.18) if cuts else 1.0
    result = jax.random.normal(rng, shape, jnp.float32) * scale * loudness
    return jnp.minimum(jnp.maximum(result, -limit), limit).astype(kind)


def setup_inputs(seed: int = 0) -> dict:
    arg_keys = jax.random.split(jax.random.key(seed), 14)
    node_feats = bell_draw(arg_keys[0], (ATOMS, C), 1.0, 6.0, ((0, 512),))
    positions = draw_positions(jax.random.fold_in(arg_keys[13], 71), 0)
    species = with_ends(jax.random.randint(arg_keys[2], (ATOMS,), 0, S), jax.random.fold_in(arg_keys[2], 1), 0, S - 1).astype(jnp.int32)
    neighbours = draw_neighbours(jax.random.fold_in(arg_keys[13], 71), 0)
    counts = with_ends(jax.random.randint(arg_keys[4], (ATOMS,), K // 4, K + 1), jax.random.fold_in(arg_keys[4], 1), K // 4, K).astype(jnp.int32)
    ghost_ids = draw_ghost_ids(jax.random.fold_in(arg_keys[13], 71), 0)
    w_node = bell_draw(arg_keys[6], (C, C), C ** -0.5, 0.5)
    w_r1 = bell_draw(arg_keys[7], (NB, HID), (NB // 2) ** -0.5, 3.0)
    w_r2 = bell_draw(arg_keys[8], (HID, HID), (HID // 2) ** -0.5, 1.0)
    w_r3 = bell_draw(arg_keys[9], (HID, HID), (HID // 2) ** -0.5, 1.0)
    w_r4 = bell_draw(arg_keys[10], (HID, 4 * C), (HID // 2) ** -0.5, 1.0)
    w_out = bell_draw(arg_keys[11], (4 * C, C), C ** -0.5, 0.5)
    species_emb = bell_draw(arg_keys[12], (S, C), 0.5, 3.0)
    return dict(node_feats=node_feats, positions=positions, species=species, neighbours=neighbours, counts=counts, ghost_ids=ghost_ids, w_node=w_node, w_r1=w_r1, w_r2=w_r2, w_r3=w_r3, w_r4=w_r4, w_out=w_out, species_emb=species_emb)


ROOT_THREE = math.sqrt(3.0)
ROOT_FIVE = math.sqrt(5.0)
ROOT_FIFTEEN = math.sqrt(15.0)
COEF_ONE = 0.5 * math.sqrt(17.5)
COEF_TWO = math.sqrt(105.0)
COEF_THREE = 0.5 * math.sqrt(10.5)
COEF_FOUR = 0.5 * math.sqrt(7.0)
COEF_FIVE = 0.5 * math.sqrt(105.0)

def harmonics(unit_x, unit_y, unit_z):
    squared = unit_x * unit_x + unit_y * unit_y + unit_z * unit_z
    degree_zero = [jnp.ones_like(unit_x)]
    degree_one = [ROOT_THREE * unit_x, ROOT_THREE * unit_y, ROOT_THREE * unit_z]
    degree_two = [ROOT_FIFTEEN * unit_x * unit_y, ROOT_FIFTEEN * unit_y * unit_z, 0.5 * ROOT_FIVE * (3.0 * unit_z * unit_z - squared), ROOT_FIFTEEN * unit_x * unit_z, 0.5 * ROOT_FIFTEEN * (unit_x * unit_x - unit_y * unit_y)]
    fifth = 5.0 * unit_z * unit_z
    degree_three = [COEF_ONE * unit_y * (3.0 * unit_x * unit_x - unit_y * unit_y), COEF_TWO * unit_x * unit_y * unit_z, COEF_THREE * unit_y * (fifth - squared), COEF_FOUR * unit_z * (fifth - 3.0 * squared), COEF_THREE * unit_x * (fifth - squared), COEF_FIVE * unit_z * (unit_x * unit_x - unit_y * unit_y), COEF_ONE * unit_x * (unit_x * unit_x - 3.0 * unit_y * unit_y)]
    return [degree_zero, degree_one, degree_two, degree_three]

def edge_invariants(sender_rows, sender_pos, centre_pos, live, w_r1, w_r2, w_r3, w_r4):
    delta = sender_pos - centre_pos[:, :, None]
    squared = lax.optimization_barrier(jnp.sum(delta * delta, axis=0))
    radius = jnp.sqrt(squared + 1.0)
    scaled = delta / radius
    nbasis = w_r1.shape[0]
    centres = 1.0 + 0.8 * jnp.arange(nbasis).astype(jnp.float32)
    basis = jnp.exp(-0.5 * (radius[..., None] - centres) ** 2).astype(jnp.bfloat16)
    atoms_blk, slots = live.shape
    layer = basis.reshape(atoms_blk * slots, nbasis)
    for weight in (w_r1, w_r2, w_r3):
        layer = jax.nn.silu(jnp.dot(layer, weight, preferred_element_type=jnp.float32)).astype(jnp.bfloat16)
    radial = jnp.dot(layer, w_r4, preferred_element_type=jnp.float32).reshape(atoms_blk, slots, 4, -1)
    weighted = radial * (sender_rows.astype(jnp.float32) * live[..., None])[:, :, None, :]
    groups = harmonics(scaled[0], scaled[1], scaled[2])
    invariants = []
    for degree in range(4):
        table = jnp.stack(groups[degree], axis=-1)
        amplitude = jnp.einsum('nkc,nkm->nmc', weighted[:, :, degree], table, precision=lax.Precision.HIGHEST)
        invariants.append(lax.optimization_barrier(jnp.sum(amplitude * amplitude, axis=1)) / (2.0 * degree + 1.0))
    return jnp.concatenate(invariants, axis=-1)

def reference(node_feats, positions, species, neighbours, counts, ghost_ids, w_node, w_r1, w_r2, w_r3, w_r4, w_out, species_emb):
    blocks_all = N_DOM * N_CH
    projected = jnp.dot(node_feats, w_node, preferred_element_type=jnp.float32).astype(jnp.bfloat16)
    grid_rows = projected.reshape(N_DOM, N_CH, A_DEV, C)
    grid_pos = positions.reshape(3, N_DOM, N_CH, A_DEV).transpose(1, 2, 3, 0)
    empty_rows = jnp.zeros((N_DOM, 1, G_DEV, C), jnp.bfloat16)
    empty_pos = jnp.zeros((N_DOM, 1, G_DEV, 3), jnp.bfloat16)
    lower_rim_rows = jnp.concatenate([empty_rows, grid_rows[:, :-1, A_DEV - G_DEV:]], axis=1)
    lower_rim_pos = jnp.concatenate([empty_pos, grid_pos[:, :-1, A_DEV - G_DEV:]], axis=1)
    upper_rim_rows = jnp.concatenate([grid_rows[:, 1:, :G_DEV], empty_rows], axis=1)
    upper_rim_pos = jnp.concatenate([grid_pos[:, 1:, :G_DEV], empty_pos], axis=1)
    ghost_index = ghost_ids.astype(jnp.int32).reshape(2, N_DOM, N_CH, G_DEV, 1)
    sent_down_rows = jnp.take_along_axis(grid_rows, ghost_index[0], axis=2)
    sent_down_pos = jnp.take_along_axis(grid_pos, ghost_index[0], axis=2)
    sent_up_rows = jnp.take_along_axis(grid_rows, ghost_index[1], axis=2)
    sent_up_pos = jnp.take_along_axis(grid_pos, ghost_index[1], axis=2)
    lower_ghost_rows = jnp.roll(sent_up_rows, 1, axis=0)
    lower_ghost_pos = jnp.roll(sent_up_pos, 1, axis=0)
    upper_ghost_rows = jnp.roll(sent_down_rows, -1, axis=0)
    upper_ghost_pos = jnp.roll(sent_down_pos, -1, axis=0)
    first_axis = jnp.array([1.0, 0.0, 0.0], jnp.float32)
    ext_rows = jnp.concatenate([lower_rim_rows, grid_rows, upper_rim_rows, lower_ghost_rows, upper_ghost_rows], axis=2).reshape(blocks_all, LOC, C)
    ext_pos = jnp.concatenate([lower_rim_pos.astype(jnp.float32), grid_pos.astype(jnp.float32), upper_rim_pos.astype(jnp.float32), lower_ghost_pos.astype(jnp.float32) - 4.0 * first_axis, upper_ghost_pos.astype(jnp.float32) + 4.0 * first_axis], axis=2).reshape(blocks_all, LOC, 3)
    live = (jnp.arange(K, dtype=jnp.int32)[None, :] < counts[:, None]).astype(jnp.float32)
    live = live.reshape(blocks_all, A_DEV, K)
    nbr_all = neighbours.astype(jnp.int32).reshape(blocks_all, A_DEV, K)
    centre_all = grid_pos.astype(jnp.float32).reshape(blocks_all, A_DEV, 3)

    def one_device(items):
        rows_dev, pos_dev, nbr_dev, live_dev, centre_dev = items
        sender_pos = jnp.transpose(pos_dev[nbr_dev], (2, 0, 1))
        return edge_invariants(rows_dev[nbr_dev], sender_pos, centre_dev.T, live_dev, w_r1, w_r2, w_r3, w_r4)
    invariants = lax.map(one_device, (ext_rows, ext_pos, nbr_all, live, centre_all))
    invariants = invariants.reshape(ATOMS, 4 * C).astype(jnp.bfloat16)
    mixed = jnp.dot(invariants, w_out, preferred_element_type=jnp.float32)
    return (mixed + species_emb[species].astype(jnp.float32)).astype(jnp.bfloat16)
```

```python
import functools
import math

import jax
import jax.numpy as jnp
from jax import lax
from jax.experimental import pallas as pl
from jax.experimental.pallas import tpu as pltpu
from jax.sharding import PartitionSpec as P

F32 = jnp.float32
BF = jnp.bfloat16
I32 = jnp.int32
MESH = pl.DeviceIdType.MESH
R3=math.sqrt(3.0);R5=math.sqrt(5.0);R15=math.sqrt(15.0)
C1=0.5*math.sqrt(17.5);C2=math.sqrt(105.0);C3=0.5*math.sqrt(10.5);C4=0.5*math.sqrt(7.0);C5=0.5*math.sqrt(105.0)

def harmonics(x,y,z):
    q=x*x+y*y+z*z
    f=5.0*z*z
    return [R3*x,R3*y,R3*z,
      R15*x*y,R15*y*z,0.5*R5*(3.0*z*z-q),R15*x*z,0.5*R15*(x*x-y*y),
      C1*y*(3.0*x*x-y*y),C2*x*y*z,C3*y*(f-q),C4*z*(f-3.0*q),C3*x*(f-q),C5*z*(x*x-y*y),C1*x*(x*x-3.0*y*y)]

def dot(a,b,ca=1,cb=0):
    return lax.dot_general(a,b,(((ca,),(cb,)),((),())),preferred_element_type=F32)

GRP=64; A=8; K=32; E=256

def st(ref,n,s,v):
    for h in range(2):
        ref.at[h][pl.ds(n,GRP,stride=s),:]=v[:,128*h:128*h+128]

def ld(ref,i,n):
    return jnp.concatenate([ref[h,pl.ds(i,n),:] for h in range(2)],axis=1)

def silu(u):
    return (u+u*jnp.tanh(u)).astype(BF)

def body(*refs,n_in,mode=3,skip=()):
    ins=refs[:n_in]; out_ref=refs[n_in]; bufs=refs[n_in+1:2*n_in+1]
    (sem,tab,nb_s,lo_s,hi_s,basis_s,y_s,inv_s,w1b,w2b,w3b,w4p,H1,H2,H3,S,W)=refs[2*n_in+1:]
    feats, pos, cnt, nbr, spec, gfeat, wn, w1, w2, w3, w4, wo, emb = ins
    (extf_ref, own_ref, cnt_ref, nbr_ref, spec_ref, gpos_ref, wn_ref, w1_ref, w2_ref, w3_ref, w4_ref, wo_ref, emb_ref) = bufs
    pairs = [(feats, extf_ref.at[pl.ds(64, 512), :]), (pos, own_ref), (cnt, cnt_ref), (nbr, nbr_ref), (spec, spec_ref)]
    for q, start in enumerate((0, 576, 640, 704)):
        pairs.append((gfeat.at[q, pl.ds(0, 64), :], extf_ref.at[pl.ds(start, 64), :]))
        pairs.append((gfeat.at[q, pl.ds(64, 16), :], gpos_ref.at[q]))
    pairs += [(wn, wn_ref), (w1, w1_ref), (w2, w2_ref), (w3, w3_ref), (w4, w4_ref), (wo, wo_ref), (emb, emb_ref)]
    cps = [pltpu.make_async_copy(x, y, sem.at[i]) for i, (x, y) in enumerate(pairs)]
    for c in cps:
        c.start()
    for c in cps:
        c.wait()
    wn=wn_ref[...]
    for t in range(3):
        tab[pl.ds(128*t,128),:]=dot(wn,extf_ref[pl.ds(256*t,256),:],0,1).astype(BF)
    r64=lax.broadcasted_iota(I32,(256,64),0)&63
    pick=jnp.where(r64==lax.broadcasted_iota(I32,(256,64),1),1.0,0.0).astype(BF)
    def spread(w,n):
        v=dot(pick,w,1,1).astype(BF)
        c=lax.broadcasted_iota(I32,(n,4*n),1)&(n-1)
        v=dot(v,jnp.where(c==lax.broadcasted_iota(I32,(n,4*n),0),1.0,0.0).astype(BF))*0.5
        same=(lax.broadcasted_iota(I32,(256,4*n),0)>>6)==(lax.broadcasted_iota(I32,(256,4*n),1)//n)
        return jnp.where(same,v,0.0).astype(BF)
    w1b[...]=spread(w1_ref[...],8)
    w2b[...]=spread(w2_ref[...],64)
    w3b[...]=spread(w3_ref[...],64)
    w4p[...]=jnp.zeros_like(w4p)
    w4p[0,pl.ds(0,64),:]=w4_ref[...]
    w4p[1,pl.ds(64,64),:]=w4_ref[...]
    nb_s[:,pl.ds(0,32)]=nbr_ref[...].T
    idx=jnp.concatenate([nb_s[pl.ds(a,GRP,stride=A),:][:,:32] for a in range(A)],axis=1)
    lo_s[...]=(idx&255).astype(F32)
    hi_s[...]=(idx>>8).astype(F32)
    atom=lax.broadcasted_iota(I32,(GRP,512),1)
    g=lax.broadcasted_iota(I32,(GRP,512),0)
    sel=(atom>>3)==g
    own=own_ref[...].astype(F32)
    rows=[own[0:1],own[1:2],own[2:3],cnt_ref[...].astype(F32)]
    M=jnp.concatenate([jnp.where(sel,rows[q],0.0).astype(BF) for q in range(4)],axis=0)
    er=lax.broadcasted_iota(I32,(512,E),0)&7
    ec=lax.broadcasted_iota(I32,(512,E),1)>>5
    X=jnp.where(er==ec,1.0,0.0).astype(BF)
    cen=dot(M,X)
    gp=[gpos_ref[q,pl.ds(0,3),:].astype(F32)[:,:64] for q in range(4)]
    ext=jnp.concatenate([gp[0],own,gp[1],gp[2],gp[3]],axis=1)
    sh=jnp.where(lax.broadcasted_iota(I32,(1,128),1)<64,-4.0,4.0)
    sp=[]
    tl=idx>>7; ll=idx&127
    for c in range(3):
        hv=[]
        for h in range(2):
            li=ll[:,128*h:128*h+128]; ti=tl[:,128*h:128*h+128]
            acc=None
            for t in range(6):
                row=ext[c:c+1,128*t:128*t+128]
                if c==0 and t==5: row=row+sh
                v=jnp.take_along_axis(jnp.broadcast_to(row,(GRP,128)),li,axis=1)
                acc=v if acc is None else jnp.where(ti==t,v,acc)
            hv.append(acc)
        sp.append(jnp.concatenate(hv,axis=1))
    d=[sp[c]-cen[64*c:64*c+64,:] for c in range(3)]
    slot=(lax.broadcasted_iota(I32,(GRP,E),1)&31).astype(F32)
    live=jnp.where(slot<cen[192:256,:],1.0,0.0)
    sq=d[0]*d[0]+d[1]*d[1]+d[2]*d[2]
    rad=jnp.sqrt(sq+1.0)
    ir=1.0/rad
    for n in range(8):
        v=rad-(1.0+0.8*n)
        st(basis_s,n,8,jnp.exp(-0.5*v*v))
    x,y,z=[a*ir for a in d]
    st(y_s,0,16,live)
    for m,v in enumerate(harmonics(x,y,z)):
        st(y_s,m+1,16,v*live)
    iota=lax.broadcasted_iota(I32,(256,E),0).astype(F32).astype(BF)
    ea=lax.broadcasted_iota(I32,(8,E),0)==(lax.broadcasted_iota(I32,(8,E),1)>>5)
    n=GRP//4
    def row(ref,i): return ref[pl.ds(i,1),:]
    def s_amp(t):
        for u in range(4):
            gi=t*4+u
            ys=[jnp.where(ea,ld(y_s,gi*16+m,1),0.0) for m in range(16)]
            ws=W[pl.ds(256*u,256),:]
            r=dot(jnp.concatenate(ys[:4],axis=0).astype(BF),ws[:,:256])
            r2=dot(jnp.concatenate(ys[4:],axis=0).astype(BF),ws[:,256:])
            amps=[r[:8,:128],r[8:,128:],r2[:40,:128],r2[40:,128:]]
            for l in range(4):
                nn=2*l+1
                sq=amps[l]*amps[l]
                tt=sq[:8]
                for m in range(1,nn): tt=tt+sq[8*m:8*m+8]
                o8=gi*8 if isinstance(gi,int) else pl.multiple_of(gi*8,8)
                inv_s[pl.ds(o8,8),pl.ds(128*l,128)]=tt*(1.0/nn)
    def s_rad(t):
        for u in range(4):
            r=dot(H3[:,pl.ds(128*(u//2),128)],w4p[u%2])
            ss=S[pl.ds(256*u,256),:].astype(F32)
            for l in range(4):
                W[pl.ds(256*u,256),pl.ds(128*l,128)]=(r[:,128*l:128*l+128]*ss).astype(BF)
    def s_gather(t):
        for u in range(4):
            lo=row(lo_s,t*4+u).astype(BF)
            hi=row(hi_s,t*4+u)
            oh=jnp.where(iota==lo,jnp.ones((),BF),jnp.zeros((),BF))
            cand=dot(tab[...],oh)
            S[pl.ds(256*u,256),:]=jnp.where(hi==0.0,cand[:128],jnp.where(hi==1.0,cand[128:256],cand[256:])).astype(BF).T
    def s_m3(t): H3[...]=silu(dot(w3b[...],H2[...])).T
    def s_m2(t): H2[...]=silu(dot(w2b[...],H1[...]))
    def s_m1(t):
        o=t*32 if isinstance(t,int) else pl.multiple_of(t*32,32)
        H1[...]=silu(dot(w1b[...],ld(basis_s,o,32).astype(BF)))
    def s_mlp(t):
        o=t*32 if isinstance(t,int) else pl.multiple_of(t*32,32)
        h=silu(dot(w1b[...],ld(basis_s,o,32).astype(BF)))
        h=silu(dot(w2b[...],h))
        H3[...]=silu(dot(w3b[...],h)).T
    if mode==3: stages=[(s_amp,2),(s_rad,1),(s_mlp,0),(s_gather,0)]
    else: stages=[(s_amp,4),(s_rad,3),(s_m3,2),(s_gather,2),(s_m2,1),(s_m1,0)]
    stages=[x for x in stages if x[0].__name__ not in skip]
    depth=max([d for _,d in stages]+[0])
    def step(t):
        for f,d in stages:
            if isinstance(t,int):
                if 0<=t-d<n: f(t-d)
            else: f(t-d)
    for t in range(depth): step(t)
    if stages:
        def stepc(t,c): step(t); return c
        lax.fori_loop(depth,n,stepc,0)
    for t in range(n,n+depth): step(t)
    oht=jnp.where(lax.broadcasted_iota(I32,(89,512),0)==spec_ref[...],1.0,0.0).astype(BF)
    out=dot(inv_s[...].astype(BF),wo_ref[...])+dot(oht,emb_ref[...],0,0)
    out_ref[...]=out.astype(BF)

def compute(*args):
    V=lambda s,d: pltpu.VMEM(s,d)
    n_in=len(args)
    bufs=[V((768,128),BF)]+[V(x.shape,x.dtype) for x in args[1:5]]+[V((4,16,128),BF)]+[V(x.shape,x.dtype) for x in args[6:]]
    return pl.pallas_call(functools.partial(body,n_in=n_in,mode=5),
        out_shape=jax.ShapeDtypeStruct((512,128),BF),
        in_specs=[pl.BlockSpec(memory_space=pl.ANY)]*n_in,
        out_specs=pl.BlockSpec(memory_space=pltpu.VMEM),
        scratch_shapes=bufs+[pltpu.SemaphoreType.DMA((20,)),V((384,256),BF),V((512,128),I32),V((64,256),F32),V((64,256),F32),V((2,512,128),F32),V((2,1024,128),F32),V((512,512),F32),
          V((256,32),BF),V((256,256),BF),V((256,256),BF),V((2,128,512),BF),V((256,256),BF),V((256,256),BF),V((256,256),BF),V((1024,128),BF),V((1024,512),BF)],
        compiler_params=pltpu.CompilerParams(vmem_limit_bytes=60*2**20),
        )(*args)


def exchange_body(feats,pos,gid,out,fbuf,pbuf,gbuf,send,sem,ssem,rsem):
    cps=[pltpu.make_async_copy(x,y,sem.at[i]) for i,(x,y) in enumerate([(feats,fbuf),(pos,pbuf),(gid,gbuf)])]
    for c in cps: c.start()
    d=lax.axis_index("dom"); j=lax.axis_index("ch")
    nd=lax.axis_size("dom"); nc=lax.axis_size("ch")
    up={"dom":lax.rem(d+1,nd)}; down={"dom":lax.rem(d+nd-1,nd)}
    nxt={"ch":lax.rem(j+1,nc)}; prv={"ch":lax.rem(j+nc-1,nc)}
    barrier=pltpu.get_barrier_semaphore()
    for to in (up,down,nxt,prv):
        pl.semaphore_signal(barrier,inc=1,device_id=to,device_id_type=MESH)
    for c in cps: c.wait()
    at=lax.broadcasted_iota(I32,(512,128),0)
    ln=lax.broadcasted_iota(I32,(512,128),1)
    pad=jnp.full((1,64),-1,I32)
    g0=jnp.concatenate([gbuf[pl.ds(0,1),:],pad],axis=1)
    g1=jnp.concatenate([gbuf[pl.ds(1,1),:],pad],axis=1)
    p16=jnp.concatenate([pbuf[...].astype(F32),jnp.zeros((13,512),F32)],axis=0).astype(BF)
    f=fbuf[...]
    sels=[(at==ln+448),(at==ln)&(ln<64),at==g0,at==g1]
    for q in range(4):
        sel=jnp.where(sels[q],1.0,0.0).astype(BF)
        send[q,pl.ds(64,16),:]=dot(p16,sel).astype(BF)
        if q==0: send[q,pl.ds(0,64),:]=f[448:]
        elif q==1: send[q,pl.ds(0,64),:]=f[:64]
        else: send[q,pl.ds(0,64),:]=dot(sel[:,:64],f,0,0).astype(BF)
    pl.semaphore_wait(barrier,4)
    def copy(q,slot,to):
        return pltpu.make_async_remote_copy(src_ref=send.at[q],dst_ref=out.at[slot],send_sem=ssem.at[q],recv_sem=rsem.at[slot],device_id=to,device_id_type=MESH)
    rc=[copy(2,3,down),copy(3,2,up),copy(0,0,nxt),copy(1,1,prv)]
    for c in rc: c.start()
    for c in rc: c.wait()
    @pl.when(j==0)
    def _(): out[0]=jnp.zeros((80,128),BF)
    @pl.when(j==nc-1)
    def _(): out[1]=jnp.zeros((80,128),BF)


def exchange(feats,pos,gid):
    V=lambda s,d: pltpu.VMEM(s,d)
    return pl.pallas_call(exchange_body,
        out_shape=jax.ShapeDtypeStruct((4,80,128),BF),
        in_specs=[pl.BlockSpec(memory_space=pl.ANY)]*3,
        out_specs=pl.BlockSpec(memory_space=pltpu.VMEM),
        scratch_shapes=[V((512,128),BF),V((3,512),BF),V((2,64),I32),V((4,80,128),BF),pltpu.SemaphoreType.DMA((3,)),pltpu.SemaphoreType.DMA((4,)),pltpu.SemaphoreType.DMA((4,))],
        compiler_params=pltpu.CompilerParams(collective_id=0,has_side_effects=True,vmem_limit_bytes=60*2**20),
        )(feats,pos,gid)


def block(node_feats,positions,species,neighbours,counts,ghost_ids,w_node,w_r1,w_r2,w_r3,w_r4,w_out,species_emb):
    ghosts=exchange(node_feats,positions,ghost_ids)
    return compute(node_feats,positions,counts.reshape(1,-1),neighbours.T,species.reshape(1,-1),ghosts,w_node,w_r1,w_r2,w_r3,w_r4,w_out,species_emb)


def solution(mesh):
    each=P(("dom","ch"),None)
    flat=P(("dom","ch"))
    cols=P(None,("dom","ch"))
    return jax.shard_map(block,mesh=mesh,
        in_specs=(each,cols,flat,each,flat,cols)+(P(),)*7,
        out_specs=each,check_vma=False)
```

```python
import functools
import math

import jax
import jax.numpy as jnp
from jax import lax
from jax.experimental import pallas as pl
from jax.experimental.pallas import tpu as pltpu
from jax.sharding import PartitionSpec as P

F32 = jnp.float32
BF = jnp.bfloat16
I32 = jnp.int32
MESH = pl.DeviceIdType.MESH
R3=math.sqrt(3.0);R5=math.sqrt(5.0);R15=math.sqrt(15.0)
C1=0.5*math.sqrt(17.5);C2=math.sqrt(105.0);C3=0.5*math.sqrt(10.5);C4=0.5*math.sqrt(7.0);C5=0.5*math.sqrt(105.0)

def harmonics(x,y,z):
    q=x*x+y*y+z*z
    f=5.0*z*z
    return [R3*x,R3*y,R3*z,
      R15*x*y,R15*y*z,0.5*R5*(3.0*z*z-q),R15*x*z,0.5*R15*(x*x-y*y),
      C1*y*(3.0*x*x-y*y),C2*x*y*z,C3*y*(f-q),C4*z*(f-3.0*q),C3*x*(f-q),C5*z*(x*x-y*y),C1*x*(x*x-3.0*y*y)]

def dot(a,b,ca=1,cb=0):
    return lax.dot_general(a,b,(((ca,),(cb,)),((),())),preferred_element_type=F32)

GRP=64; A=8; K=32; E=256

def st(ref,n,s,v):
    for h in range(2):
        ref.at[h][pl.ds(n,GRP,stride=s),:]=v[:,128*h:128*h+128]

def ld(ref,i,n):
    return jnp.concatenate([ref[h,pl.ds(i,n),:] for h in range(2)],axis=1)

def silu(u):
    return (u+u*jnp.tanh(u)).astype(BF)

def body(*refs,n_in):
    ins=refs[:n_in]; out_ref=refs[n_in]; bufs=refs[n_in+1:2*n_in+1]
    (extf,send,recv,sem,ssem,rsem,tab,nb_s,lo_s,hi_s,basis_s,y_s,inv_s,w1b,w2b,w3b,w4p,H1,H2,H3,S,W)=refs[2*n_in+1:]
    d=lax.axis_index("dom"); j=lax.axis_index("ch")
    nd=lax.axis_size("dom"); nc=lax.axis_size("ch")
    up={"dom":lax.rem(d+1,nd)}; down={"dom":lax.rem(d+nd-1,nd)}
    nxt={"ch":lax.rem(j+1,nc)}; prv={"ch":lax.rem(j+nc-1,nc)}
    barrier=pltpu.get_barrier_semaphore()
    for to in (up,down,nxt,prv):
        pl.semaphore_signal(barrier,inc=1,device_id=to,device_id_type=MESH)
    cps=[pltpu.make_async_copy(x,y,sem.at[i]) for i,(x,y) in enumerate(zip(ins,bufs))]
    for c in cps: c.start()
    f_ref,own_ref,gid_ref,cnt_ref,nbr_ref,spec_ref,wn_ref,w1_ref,w2_ref,w3_ref,w4_ref,wo_ref,emb_ref=bufs
    for c in cps[:3]: c.wait()
    at=lax.broadcasted_iota(I32,(512,128),0)
    ln=lax.broadcasted_iota(I32,(512,128),1)
    pad=jnp.full((1,64),-1,I32)
    g0=jnp.concatenate([gid_ref[pl.ds(0,1),:],pad],axis=1)
    g1=jnp.concatenate([gid_ref[pl.ds(1,1),:],pad],axis=1)
    p16=jnp.concatenate([own_ref[...].astype(F32),jnp.zeros((13,512),F32)],axis=0).astype(BF)
    f=f_ref[...]
    sels=[(at==ln+448),(at==ln)&(ln<64),at==g0,at==g1]
    for q in range(4):
        sl=jnp.where(sels[q],1.0,0.0).astype(BF)
        send[q,pl.ds(64,16),:]=dot(p16,sl).astype(BF)
        if q==0: send[q,pl.ds(0,64),:]=f[448:]
        elif q==1: send[q,pl.ds(0,64),:]=f[:64]
        else: send[q,pl.ds(0,64),:]=dot(sl[:,:64],f,0,0).astype(BF)
    pl.semaphore_wait(barrier,4)
    def copy(q,slot,to):
        return pltpu.make_async_remote_copy(src_ref=send.at[q],dst_ref=recv.at[slot],send_sem=ssem.at[q],recv_sem=rsem.at[slot],device_id=to,device_id_type=MESH)
    rc=[copy(2,3,down),copy(3,2,up),copy(0,0,nxt),copy(1,1,prv)]
    for c in rc: c.start()
    for c in cps[3:]: c.wait()
    extf[pl.ds(64,512),:]=f
    r64=lax.broadcasted_iota(I32,(256,64),0)&63
    pick=jnp.where(r64==lax.broadcasted_iota(I32,(256,64),1),1.0,0.0).astype(BF)
    def spread(w,n):
        v=dot(pick,w,1,1).astype(BF)
        c=lax.broadcasted_iota(I32,(n,4*n),1)&(n-1)
        v=dot(v,jnp.where(c==lax.broadcasted_iota(I32,(n,4*n),0),1.0,0.0).astype(BF))*0.5
        same=(lax.broadcasted_iota(I32,(256,4*n),0)>>6)==(lax.broadcasted_iota(I32,(256,4*n),1)//n)
        return jnp.where(same,v,0.0).astype(BF)
    w1b[...]=spread(w1_ref[...],8)
    w2b[...]=spread(w2_ref[...],64)
    w3b[...]=spread(w3_ref[...],64)
    w4p[...]=jnp.zeros_like(w4p)
    w4p[0,pl.ds(0,64),:]=w4_ref[...]
    w4p[1,pl.ds(64,64),:]=w4_ref[...]
    nb_s[:,pl.ds(0,32)]=nbr_ref[...].T
    idx=jnp.concatenate([nb_s[pl.ds(a,GRP,stride=A),:][:,:32] for a in range(A)],axis=1)
    lo_s[...]=(idx&255).astype(F32)
    hi_s[...]=(idx>>8).astype(F32)
    atom=lax.broadcasted_iota(I32,(GRP,512),1)
    g=lax.broadcasted_iota(I32,(GRP,512),0)
    sel=(atom>>3)==g
    own=own_ref[...].astype(F32)
    rows=[own[0:1],own[1:2],own[2:3],cnt_ref[...].astype(F32)]
    M=jnp.concatenate([jnp.where(sel,rows[q],0.0).astype(BF) for q in range(4)],axis=0)
    er=lax.broadcasted_iota(I32,(512,E),0)&7
    ec=lax.broadcasted_iota(I32,(512,E),1)>>5
    X=jnp.where(er==ec,1.0,0.0).astype(BF)
    cen=dot(M,X)
    tl=idx>>7; ll=idx&127
    def gather(acc,tiles,table):
        for c in range(3):
            for h in range(2):
                li=ll[:,128*h:128*h+128]; ti=tl[:,128*h:128*h+128]
                for t in tiles:
                    rw=table(c,t)
                    v=jnp.take_along_axis(jnp.broadcast_to(rw,(GRP,128)),li,axis=1)
                    acc[c][h]=v if acc[c][h] is None else jnp.where(ti==t,v,acc[c][h])
        return acc
    acc=gather([[None,None] for _ in range(3)],(1,2,3),lambda c,t: own[c:c+1,128*t-64:128*t+64])
    wn=wn_ref[...]
    tab[pl.ds(128,128),:]=dot(wn,extf[pl.ds(256,256),:],0,1).astype(BF)
    iota=lax.broadcasted_iota(I32,(256,E),0).astype(F32).astype(BF)
    ea=lax.broadcasted_iota(I32,(8,E),0)==(lax.broadcasted_iota(I32,(8,E),1)>>5)
    for c in rc: c.wait()
    @pl.when(j==0)
    def _(): recv[0]=jnp.zeros((80,128),BF)
    @pl.when(j==nc-1)
    def _(): recv[1]=jnp.zeros((80,128),BF)
    for q,start in enumerate((0,576,640,704)):
        extf[pl.ds(start,64),:]=recv[q,pl.ds(0,64),:]
    for t in (0,2):
        tab[pl.ds(128*t,128),:]=dot(wn,extf[pl.ds(256*t,256),:],0,1).astype(BF)
    gp=[recv[q,pl.ds(64,16),:].astype(F32)[:3,:64] for q in range(4)]
    ext=jnp.concatenate([gp[0],own,gp[1],gp[2],gp[3]],axis=1)
    sh=jnp.where(lax.broadcasted_iota(I32,(1,128),1)<64,-4.0,4.0)
    acc=gather(acc,(0,4,5),lambda c,t: ext[c:c+1,128*t:128*t+128]+(sh if c==0 and t==5 else 0.0))
    sp=[jnp.concatenate(acc[c],axis=1) for c in range(3)]
    d=[sp[c]-cen[64*c:64*c+64,:] for c in range(3)]
    slot=(lax.broadcasted_iota(I32,(GRP,E),1)&31).astype(F32)
    live=jnp.where(slot<cen[192:256,:],1.0,0.0)
    sq=d[0]*d[0]+d[1]*d[1]+d[2]*d[2]
    rad=jnp.sqrt(sq+1.0)
    ir=1.0/rad
    for n in range(8):
        v=rad-(1.0+0.8*n)
        st(basis_s,n,8,jnp.exp(-0.5*v*v))
    x,y,z=[a*ir for a in d]
    st(y_s,0,16,live)
    for m,v in enumerate(harmonics(x,y,z)):
        st(y_s,m+1,16,v*live)
    n=GRP//4
    def row(ref,i): return ref[pl.ds(i,1),:]
    def s_amp(t):
        for u in range(4):
            gi=t*4+u
            ys=[jnp.where(ea,ld(y_s,gi*16+m,1),0.0) for m in range(16)]
            ws=W[pl.ds(256*u,256),:]
            r=dot(jnp.concatenate(ys[:4],axis=0).astype(BF),ws[:,:256])
            r2=dot(jnp.concatenate(ys[4:],axis=0).astype(BF),ws[:,256:])
            amps=[r[:8,:128],r[8:,128:],r2[:40,:128],r2[40:,128:]]
            for l in range(4):
                nn=2*l+1
                sq=amps[l]*amps[l]
                tt=sq[:8]
                for m in range(1,nn): tt=tt+sq[8*m:8*m+8]
                o8=gi*8 if isinstance(gi,int) else pl.multiple_of(gi*8,8)
                inv_s[pl.ds(o8,8),pl.ds(128*l,128)]=tt*(1.0/nn)
    def s_rad(t):
        for u in range(4):
            r=dot(H3[:,pl.ds(128*(u//2),128)],w4p[u%2])
            ss=S[pl.ds(256*u,256),:].astype(F32)
            for l in range(4):
                W[pl.ds(256*u,256),pl.ds(128*l,128)]=(r[:,128*l:128*l+128]*ss).astype(BF)
    def s_gather(t):
        for u in range(4):
            lo=row(lo_s,t*4+u).astype(BF)
            hi=row(hi_s,t*4+u)
            oh=jnp.where(iota==lo,jnp.ones((),BF),jnp.zeros((),BF))
            cand=dot(tab[...],oh)
            S[pl.ds(256*u,256),:]=jnp.where(hi==0.0,cand[:128],jnp.where(hi==1.0,cand[128:256],cand[256:])).astype(BF).T
    def s_m3(t): H3[...]=silu(dot(w3b[...],H2[...])).T
    def s_m2(t): H2[...]=silu(dot(w2b[...],H1[...]))
    def s_m1(t):
        o=t*32 if isinstance(t,int) else pl.multiple_of(t*32,32)
        H1[...]=silu(dot(w1b[...],ld(basis_s,o,32).astype(BF)))
    stages=[(s_amp,4),(s_rad,3),(s_m3,2),(s_gather,2),(s_m2,1),(s_m1,0)]
    depth=4
    def step(t):
        for f,d in stages:
            if isinstance(t,int):
                if 0<=t-d<n: f(t-d)
            else: f(t-d)
    for t in range(depth): step(t)
    def stepc(t,c): step(t); return c
    lax.fori_loop(depth,n,stepc,0)
    for t in range(n,n+depth): step(t)
    oht=jnp.where(lax.broadcasted_iota(I32,(89,512),0)==spec_ref[...],1.0,0.0).astype(BF)
    out=dot(inv_s[...].astype(BF),wo_ref[...])+dot(oht,emb_ref[...],0,0)
    out_ref[...]=out.astype(BF)

def block(node_feats,positions,species,neighbours,counts,ghost_ids,w_node,w_r1,w_r2,w_r3,w_r4,w_out,species_emb):
    args=(node_feats,positions,ghost_ids,counts.reshape(1,-1),neighbours.T,species.reshape(1,-1),w_node,w_r1,w_r2,w_r3,w_r4,w_out,species_emb)
    V=lambda s,d: pltpu.VMEM(s,d)
    n_in=len(args)
    return pl.pallas_call(functools.partial(body,n_in=n_in),
        out_shape=jax.ShapeDtypeStruct((512,128),BF),
        in_specs=[pl.BlockSpec(memory_space=pl.ANY)]*n_in,
        out_specs=pl.BlockSpec(memory_space=pltpu.VMEM),
        scratch_shapes=[V(x.shape,x.dtype) for x in args]+[V((768,128),BF),V((4,80,128),BF),V((4,80,128),BF),
          pltpu.SemaphoreType.DMA((n_in,)),pltpu.SemaphoreType.DMA((4,)),pltpu.SemaphoreType.DMA((4,)),V((384,256),BF),V((512,128),I32),V((64,256),F32),V((64,256),F32),V((2,512,128),F32),V((2,1024,128),F32),V((512,512),F32),
          V((256,32),BF),V((256,256),BF),V((256,256),BF),V((2,128,512),BF),V((256,256),BF),V((256,256),BF),V((256,256),BF),V((1024,128),BF),V((1024,512),BF)],
        compiler_params=pltpu.CompilerParams(collective_id=0,has_side_effects=True,vmem_limit_bytes=60*2**20),
        )(*args)


def solution(mesh):
    each=P(("dom","ch"),None)
    flat=P(("dom","ch"))
    cols=P(None,("dom","ch"))
    return jax.shard_map(block,mesh=mesh,
        in_specs=(each,cols,flat,each,flat,cols)+(P(),)*7,
        out_specs=each,check_vma=False)
```

```python
import functools
import math

import jax
import jax.numpy as jnp
from jax import lax
from jax.experimental import pallas as pl
from jax.experimental.pallas import tpu as pltpu
from jax.sharding import PartitionSpec as P

F32 = jnp.float32
BF = jnp.bfloat16
I32 = jnp.int32
MESH = pl.DeviceIdType.MESH
R3=math.sqrt(3.0);R5=math.sqrt(5.0);R15=math.sqrt(15.0)
C1=0.5*math.sqrt(17.5);C2=math.sqrt(105.0);C3=0.5*math.sqrt(10.5);C4=0.5*math.sqrt(7.0);C5=0.5*math.sqrt(105.0)

def harmonics(x,y,z):
    q=x*x+y*y+z*z
    f=5.0*z*z
    return [R3*x,R3*y,R3*z,
      R15*x*y,R15*y*z,0.5*R5*(3.0*z*z-q),R15*x*z,0.5*R15*(x*x-y*y),
      C1*y*(3.0*x*x-y*y),C2*x*y*z,C3*y*(f-q),C4*z*(f-3.0*q),C3*x*(f-q),C5*z*(x*x-y*y),C1*x*(x*x-3.0*y*y)]

def dot(a,b,ca=1,cb=0):
    return lax.dot_general(a,b,(((ca,),(cb,)),((),())),preferred_element_type=F32)

FREE=8
GRP=64; A=8; K=32; E=256

def ld(ref,i,n):
    return jnp.concatenate([ref[h,pl.ds(i,n),:] for h in range(2)],axis=1)

def silu(u):
    return (u+u*jnp.tanh(u)).astype(BF)

def weights(w1_ref,w2_ref,w3_ref,w4_ref,w1b,w2b,w3b,w4p):
    r64=lax.broadcasted_iota(I32,(256,64),0)&63
    pick=jnp.where(r64==lax.broadcasted_iota(I32,(256,64),1),1.0,0.0).astype(BF)
    def spread(w,n):
        v=dot(pick,w,1,1).astype(BF)
        c=lax.broadcasted_iota(I32,(n,4*n),1)&(n-1)
        v=dot(v,jnp.where(c==lax.broadcasted_iota(I32,(n,4*n),0),1.0,0.0).astype(BF))*0.5
        same=(lax.broadcasted_iota(I32,(256,4*n),0)>>6)==(lax.broadcasted_iota(I32,(256,4*n),1)//n)
        return jnp.where(same,v,0.0).astype(BF)
    w1b[...]=spread(w1_ref[...],8)
    w2b[...]=spread(w2_ref[...],64)
    w3b[...]=spread(w3_ref[...],64)
    w4p[...]=jnp.zeros_like(w4p)
    w4p[0,pl.ds(0,64),:]=w4_ref[...]
    w4p[1,pl.ds(64,64),:]=w4_ref[...]


def pipeline(first,n,refs):
    tab,lo_s,hi_s,basis_s,y_s,inv_s,w1b,w2b,w3b,w4p,H1,H2,H3,S,W=refs
    iota=lax.broadcasted_iota(I32,(256,E),0).astype(F32).astype(BF)
    ea=lax.broadcasted_iota(I32,(8,E),0)==(lax.broadcasted_iota(I32,(8,E),1)>>5)
    def row(ref,i): return ref[pl.ds(i,1),:]
    def s_amp(t):
        for u in range(4):
            gi=t*4+u
            ys=[jnp.where(ea,ld(y_s,gi*16+m,1),0.0) for m in range(16)]
            ws=W[pl.ds(256*u,256),:]
            r=dot(jnp.concatenate(ys[:4],axis=0).astype(BF),ws[:,:256])
            r2=dot(jnp.concatenate(ys[4:],axis=0).astype(BF),ws[:,256:])
            amps=[r[:8,:128],r[8:,128:],r2[:40,:128],r2[40:,128:]]
            for l in range(4):
                nn=2*l+1
                sq=amps[l]*amps[l]
                tt=sq[:8]
                for m in range(1,nn): tt=tt+sq[8*m:8*m+8]
                o8=gi*8 if isinstance(gi,int) else pl.multiple_of(gi*8,8)
                inv_s[pl.ds(o8,8),pl.ds(128*l,128)]=tt*(1.0/nn)
    def s_rad(t):
        for u in range(4):
            r=dot(H3[:,pl.ds(128*(u//2),128)],w4p[u%2])
            ss=S[pl.ds(256*u,256),:].astype(F32)
            for l in range(4):
                W[pl.ds(256*u,256),pl.ds(128*l,128)]=(r[:,128*l:128*l+128]*ss).astype(BF)
    def s_gather(t):
        for u in range(4):
            lo=row(lo_s,t*4+u).astype(BF)
            hi=row(hi_s,t*4+u)
            oh=jnp.where(iota==lo,jnp.ones((),BF),jnp.zeros((),BF))
            cand=dot(tab[...],oh)
            S[pl.ds(256*u,256),:]=jnp.where(hi==0.0,cand[:128],jnp.where(hi==1.0,cand[128:256],cand[256:])).astype(BF).T
    def s_m3(t): H3[...]=silu(dot(w3b[...],H2[...])).T
    def s_m2(t): H2[...]=silu(dot(w2b[...],H1[...]))
    def s_m1(t):
        o=t*32 if isinstance(t,int) else pl.multiple_of(t*32,32)
        H1[...]=silu(dot(w1b[...],ld(basis_s,o,32).astype(BF)))
    stages=[(s_amp,4),(s_rad,3),(s_m3,2),(s_gather,2),(s_m2,1),(s_m1,0)]
    depth=min(4,n)
    def step(t):
        for f,d in stages:
            if isinstance(t,int):
                if 0<=t-d<n: f(t-d+first)
            else: f(t-d+first)
    for t in range(depth): step(t)
    def stepc(t,c): step(t); return c
    lax.fori_loop(depth,n,stepc,0)
    for t in range(n,n+depth): step(t)


def mix(inv_s,wo_ref,spec,emb_ref):
    oht=jnp.where(lax.broadcasted_iota(I32,(emb_ref.shape[0],512),0)==spec,1.0,0.0).astype(BF)
    return (dot(inv_s[...].astype(BF),wo_ref[...])+dot(oht,emb_ref[...],0,0)).astype(BF)


def gather(acc,tl,ll,tiles,table):
    for c in range(3):
        for h in range(2):
            li=ll[:,128*h:128*h+128]; ti=tl[:,128*h:128*h+128]
            for t in tiles:
                v=jnp.take_along_axis(jnp.broadcast_to(table(c,t),li.shape),li,axis=1)
                acc[c][h]=v if acc[c][h] is None else jnp.where(ti==t,v,acc[c][h])
    return acc


def geometry(acc,cen,first,basis_s,y_s):
    n=cen[0].shape[0]
    d=[jnp.concatenate(acc[c],axis=1)-cen[c] for c in range(3)]
    slot=(lax.broadcasted_iota(I32,(n,E),1)&31).astype(F32)
    live=jnp.where(slot<cen[3],1.0,0.0)
    rad=jnp.sqrt(d[0]*d[0]+d[1]*d[1]+d[2]*d[2]+1.0)
    ir=1.0/rad
    def st(ref,at,s,v):
        for h in range(2):
            ref.at[h][pl.ds(first*s+at,n,stride=s),:]=v[:,128*h:128*h+128]
    for k in range(8):
        v=rad-(1.0+0.8*k)
        st(basis_s,k,8,jnp.exp(-0.5*v*v))
    x,y,z=[a*ir for a in d]
    st(y_s,0,16,live)
    for m,v in enumerate(harmonics(x,y,z)):
        st(y_s,m+1,16,v*live)


def per_edge(rows):
    atom=lax.broadcasted_iota(I32,(GRP,512),1)
    g=lax.broadcasted_iota(I32,(GRP,512),0)
    sel=(atom>>3)==g
    M=jnp.concatenate([jnp.where(sel,r,0.0).astype(BF) for r in rows],axis=0)
    er=lax.broadcasted_iota(I32,(512,E),0)&7
    ec=lax.broadcasted_iota(I32,(512,E),1)>>5
    return dot(M,jnp.where(er==ec,1.0,0.0).astype(BF))


def whole(ins,out_ref,bufs,scratch):
    sem,tab,nb_s,lo_s,hi_s,basis_s,y_s,inv_s,w1b,w2b,w3b,w4p,H1,H2,H3,S,W=scratch
    feats, pos, cnt, nbr, spec, gfeat, wn, w1, w2, w3, w4, wo, emb = ins
    (extf_ref, own_ref, cnt_ref, nbr_ref, spec_ref, gpos_ref, wn_ref, w1_ref, w2_ref, w3_ref, w4_ref, wo_ref, emb_ref) = bufs
    pairs = [(feats, extf_ref.at[pl.ds(64, 512), :]), (pos, own_ref), (cnt, cnt_ref), (nbr, nbr_ref), (spec, spec_ref)]
    for q, start in enumerate((0, 576, 640, 704)):
        pairs.append((gfeat.at[q, pl.ds(0, 64), :], extf_ref.at[pl.ds(start, 64), :]))
        pairs.append((gfeat.at[q, pl.ds(64, 16), :], gpos_ref.at[q]))
    pairs += [(wn, wn_ref), (w1, w1_ref), (w2, w2_ref), (w3, w3_ref), (w4, w4_ref), (wo, wo_ref), (emb, emb_ref)]
    cps = [pltpu.make_async_copy(x, y, sem.at[i]) for i, (x, y) in enumerate(pairs)]
    for c in cps:
        c.start()
    for c in cps:
        c.wait()
    wn=wn_ref[...]
    for t in range(3):
        tab[pl.ds(128*t,128),:]=dot(wn,extf_ref[pl.ds(256*t,256),:],0,1).astype(BF)
    weights(w1_ref,w2_ref,w3_ref,w4_ref,w1b,w2b,w3b,w4p)
    nb_s[:,pl.ds(0,32)]=nbr_ref[...].T
    idx=jnp.concatenate([nb_s[pl.ds(a,GRP,stride=A),:][:,:32] for a in range(A)],axis=1)
    lo_s[...]=(idx&255).astype(F32)
    hi_s[...]=(idx>>8).astype(F32)
    own=own_ref[...].astype(F32)
    cen=per_edge([own[0:1],own[1:2],own[2:3],cnt_ref[...].astype(F32)])
    gp=[gpos_ref[q,pl.ds(0,3),:].astype(F32)[:,:64] for q in range(4)]
    ext=jnp.concatenate([gp[0],own,gp[1],gp[2],gp[3]],axis=1)
    sh=jnp.where(lax.broadcasted_iota(I32,(1,128),1)<64,-4.0,4.0)
    acc=gather([[None,None] for _ in range(3)],idx>>7,idx&127,range(6),lambda c,t: ext[c:c+1,128*t:128*t+128]+(sh if c==0 and t==5 else 0.0))
    geometry(acc,[cen[64*c:64*c+64] for c in range(4)],0,basis_s,y_s)
    pipeline(0,GRP//4,(tab,lo_s,hi_s,basis_s,y_s,inv_s,w1b,w2b,w3b,w4p,H1,H2,H3,S,W))
    out_ref[...]=mix(inv_s,wo_ref,spec_ref[...],emb_ref)


def body(*refs,n_in):
    ins=refs[:n_in]; out_ref,recv,nf_ref=refs[n_in:n_in+3]; bufs=refs[n_in+3:2*n_in+3]
    (extf,send,perm,sem,ssem,rsem,tab,nb_s,lo_s,hi_s,basis_s,y_s,inv_s,w1b,w2b,w3b,w4p,H1,H2,H3,S,W)=refs[2*n_in+3:]
    d=lax.axis_index("dom"); j=lax.axis_index("ch")
    nd=lax.axis_size("dom"); nc=lax.axis_size("ch")
    up={"dom":lax.rem(d+1,nd)}; down={"dom":lax.rem(d+nd-1,nd)}
    nxt={"ch":lax.rem(j+1,nc)}; prv={"ch":lax.rem(j+nc-1,nc)}
    barrier=pltpu.get_barrier_semaphore()
    for to in (up,down,nxt,prv):
        pl.semaphore_signal(barrier,inc=1,device_id=to,device_id_type=MESH)
    cps=[pltpu.make_async_copy(x,y,sem.at[i]) for i,(x,y) in enumerate(zip(ins,bufs))]
    for c in cps: c.start()
    f_ref,own_ref,gid_ref,cnt_ref,nbr_ref,spec_ref,wn_ref,w1_ref,w2_ref,w3_ref,w4_ref,wo_ref,emb_ref=bufs
    for c in cps[:3]: c.wait()
    at=lax.broadcasted_iota(I32,(512,128),0)
    ln=lax.broadcasted_iota(I32,(512,128),1)
    pad=jnp.full((1,64),-1,I32)
    g0=jnp.concatenate([gid_ref[pl.ds(0,1),:],pad],axis=1)
    g1=jnp.concatenate([gid_ref[pl.ds(1,1),:],pad],axis=1)
    p16=jnp.concatenate([own_ref[...].astype(F32),jnp.zeros((13,512),F32)],axis=0).astype(BF)
    f=f_ref[...]
    sels=[(at==ln+448),(at==ln)&(ln<64),at==g0,at==g1]
    for q in range(4):
        sl=jnp.where(sels[q],1.0,0.0).astype(BF)
        send[q,pl.ds(64,16),:]=dot(p16,sl).astype(BF)
        if q==0: send[q,pl.ds(0,64),:]=f[448:]
        elif q==1: send[q,pl.ds(0,64),:]=f[:64]
        else: send[q,pl.ds(0,64),:]=dot(sl[:,:64],f,0,0).astype(BF)
    pl.semaphore_wait(barrier,4)
    def copy(q,slot,to):
        return pltpu.make_async_remote_copy(src_ref=send.at[q],dst_ref=recv.at[slot],send_sem=ssem.at[q],recv_sem=rsem.at[slot],device_id=to,device_id_type=MESH)
    rc=[copy(2,3,down),copy(3,2,up),copy(0,0,nxt),copy(1,1,prv)]
    for c in rc: c.start()
    for c in cps[3:]: c.wait()
    extf[pl.ds(0,64),:]=jnp.zeros((64,128),BF)
    extf[pl.ds(576,192),:]=jnp.zeros((192,128),BF)
    extf[pl.ds(64,512),:]=f
    wn=wn_ref[...]
    def table(t):
        tab[pl.ds(128*t,128),:]=dot(wn,extf[pl.ds(256*t,256),:],0,1).astype(BF)
    for t in range(3): table(t)
    nb=nbr_ref[...]
    cnt=cnt_ref[...]
    far=((nb<64)|(nb>=576))&(lax.broadcasted_iota(I32,(K,512),0)<cnt)
    free=1.0-jnp.max(jnp.where(far,1.0,0.0),axis=0,keepdims=True)
    ra=lax.broadcasted_iota(I32,(512,512),0)
    ca=lax.broadcasted_iota(I32,(512,512),1)
    below=jnp.where(ra<ca,1.0,0.0).astype(BF)
    before=dot(jnp.broadcast_to(free,(8,512)).astype(BF),below)[0:1]
    total=jnp.sum(free,axis=1,keepdims=True)
    nf_ref[...]=jnp.broadcast_to(total,(8,128))
    place=jnp.where(free>0.5,before,total+ca[0:1].astype(F32)-before)
    pm=jnp.where(ra==place.astype(I32),1.0,0.0).astype(BF)
    perm[...]=pm.T
    own=own_ref[...].astype(F32)
    R=jnp.concatenate([(nb&255).astype(F32),(nb>>8).astype(F32),own,cnt.astype(F32),spec_ref[...].astype(F32),jnp.zeros((59,512),F32)],axis=0).astype(BF)
    moved=dot(pm,R,1,1)
    nb_s[...]=moved
    atoms=moved.T[64:72]
    parts=[nb_s[pl.ds(a,GRP,stride=A),:] for a in range(A)]
    lo=jnp.concatenate([p[:,:32] for p in parts],axis=1)
    hi=jnp.concatenate([p[:,32:64] for p in parts],axis=1)
    lo_s[...]=lo
    hi_s[...]=hi
    lo=lo.astype(I32)
    tl=hi.astype(I32)*2+(lo>>7); ll=lo&127
    cen=per_edge([atoms[q:q+1] for q in range(4)])
    weights(w1_ref,w2_ref,w3_ref,w4_ref,w1b,w2b,w3b,w4p)
    zero=jnp.zeros((1,64),F32)
    near=jnp.concatenate([jnp.concatenate([zero,own[c:c+1],zero],axis=1) for c in range(3)],axis=0)
    G=4*FREE
    first=lambda x: x[:G]
    acc=gather([[None,None] for _ in range(3)],first(tl),first(ll),range(5),lambda c,t: near[c:c+1,128*t:128*t+128])
    geometry(acc,[cen[64*c:64*c+G] for c in range(4)],0,basis_s,y_s)
    work=(tab,lo_s,hi_s,basis_s,y_s,inv_s,w1b,w2b,w3b,w4p,H1,H2,H3,S,W)
    pipeline(0,FREE,work)
    acc=gather([[None,None] for _ in range(3)],tl[G:],ll[G:],(1,2,3),lambda c,t: near[c:c+1,128*t:128*t+128])
    for c in rc: c.wait()
    @pl.when(j==0)
    def _(): recv[0]=jnp.zeros((80,128),BF)
    @pl.when(j==nc-1)
    def _(): recv[1]=jnp.zeros((80,128),BF)
    for q,start in enumerate((0,576,640,704)):
        extf[pl.ds(start,64),:]=recv[q,pl.ds(0,64),:]
    for t in (0,2): table(t)
    gp=[recv[q,pl.ds(64,16),:].astype(F32)[:3,:64] for q in range(4)]
    ext=jnp.concatenate([gp[0],own,gp[1],gp[2],gp[3]],axis=1)
    sh=jnp.where(lax.broadcasted_iota(I32,(1,128),1)<64,-4.0,4.0)
    acc=gather(acc,tl[G:],ll[G:],(0,4,5),lambda c,t: ext[c:c+1,128*t:128*t+128]+(sh if c==0 and t==5 else 0.0))
    geometry(acc,[cen[64*c+G:64*c+64] for c in range(4)],G,basis_s,y_s)
    pipeline(FREE,GRP//4-FREE,work)
    res=mix(inv_s,wo_ref,atoms[4:5].astype(I32),emb_ref)
    out_ref[...]=dot(perm[...],res).astype(BF)


def finish_body(*refs,n_in):
    done,nf=refs[:2]; ins=refs[2:n_in]; out=refs[n_in]
    nfb,sems=refs[n_in+1:n_in+3]; bufs=refs[n_in+3:2*n_in+1]; scratch=refs[2*n_in+1:]
    one=pltpu.make_async_copy(nf,nfb,sems.at[0])
    two=pltpu.make_async_copy(done,out,sems.at[1])
    one.start(); two.start()
    one.wait(); two.wait()
    @pl.when(jnp.max(nfb[...])<32.0*FREE)
    def _(): whole(ins,out,bufs,scratch)


def block(node_feats,positions,species,neighbours,counts,ghost_ids,w_node,w_r1,w_r2,w_r3,w_r4,w_out,species_emb):
    V=pltpu.VMEM
    common=[V((384,256),BF),V((512,128),F32),V((64,256),F32),V((64,256),F32),V((2,512,128),F32),V((2,1024,128),F32),V((512,512),F32),
          V((256,32),BF),V((256,256),BF),V((256,256),BF),V((2,128,512),BF),V((256,256),BF),V((256,256),BF),V((256,256),BF),V((1024,128),BF),V((1024,512),BF)]
    counts=counts.reshape(1,-1); species=species.reshape(1,-1); neighbours=neighbours.T
    ws=(w_node,w_r1,w_r2,w_r3,w_r4,w_out,species_emb)
    args=(node_feats,positions,ghost_ids,counts,neighbours,species)+ws
    n_in=len(args)
    done,ghosts,free=pl.pallas_call(functools.partial(body,n_in=n_in),
        out_shape=[jax.ShapeDtypeStruct((512,128),BF),jax.ShapeDtypeStruct((4,80,128),BF),jax.ShapeDtypeStruct((8,128),F32)],
        in_specs=[pl.BlockSpec(memory_space=pl.ANY)]*n_in,
        out_specs=[pl.BlockSpec(memory_space=pltpu.VMEM)]*3,
        scratch_shapes=[V(x.shape,x.dtype) for x in args]+[V((768,128),BF),V((4,80,128),BF),V((512,512),BF),
          pltpu.SemaphoreType.DMA((n_in,)),pltpu.SemaphoreType.DMA((4,)),pltpu.SemaphoreType.DMA((4,)),V((384,256),BF),V((512,128),F32),V((64,256),F32),V((64,256),F32),V((2,512,128),F32),V((2,1024,128),F32),V((512,512),F32),
          V((256,32),BF),V((256,256),BF),V((256,256),BF),V((2,128,512),BF),V((256,256),BF),V((256,256),BF),V((256,256),BF),V((1024,128),BF),V((1024,512),BF)],
        compiler_params=pltpu.CompilerParams(collective_id=0,has_side_effects=True,vmem_limit_bytes=60*2**20),
        )(*args)
    args=(done,free,node_feats,positions,counts,neighbours,species,ghosts)+ws
    n_in=len(args)
    bufs=[V((768,128),BF)]+[V(x.shape,x.dtype) for x in args[3:7]]+[V((4,16,128),BF)]+[V(x.shape,x.dtype) for x in ws]
    return pl.pallas_call(functools.partial(finish_body,n_in=n_in),
        out_shape=jax.ShapeDtypeStruct((512,128),BF),
        in_specs=[pl.BlockSpec(memory_space=pl.ANY)]*n_in,
        out_specs=pl.BlockSpec(memory_space=pltpu.VMEM),
        scratch_shapes=[V((8,128),F32),pltpu.SemaphoreType.DMA((2,))]+bufs+[pltpu.SemaphoreType.DMA((20,)),V((384,256),BF),V((512,128),I32),V((64,256),F32),V((64,256),F32),V((2,512,128),F32),V((2,1024,128),F32),V((512,512),F32),
          V((256,32),BF),V((256,256),BF),V((256,256),BF),V((2,128,512),BF),V((256,256),BF),V((256,256),BF),V((256,256),BF),V((1024,128),BF),V((1024,512),BF)],
        compiler_params=pltpu.CompilerParams(vmem_limit_bytes=60*2**20),
        )(*args)


def solution(mesh):
    each=P(("dom","ch"),None)
    flat=P(("dom","ch"))
    cols=P(None,("dom","ch"))
    return jax.shard_map(block,mesh=mesh,
        in_specs=(each,cols,flat,each,flat,cols)+(P(),)*7,
        out_specs=each,check_vma=False)
```

```python
import functools
import math

import jax
import jax.numpy as jnp
from jax import lax
from jax.experimental import pallas as pl
from jax.experimental.pallas import tpu as pltpu
from jax.sharding import PartitionSpec as P

F32 = jnp.float32
BF = jnp.bfloat16
I32 = jnp.int32
MESH = pl.DeviceIdType.MESH
R3=math.sqrt(3.0);R5=math.sqrt(5.0);R15=math.sqrt(15.0)
C1=0.5*math.sqrt(17.5);C2=math.sqrt(105.0);C3=0.5*math.sqrt(10.5);C4=0.5*math.sqrt(7.0);C5=0.5*math.sqrt(105.0)

def harmonics(x,y,z):
    q=x*x+y*y+z*z
    f=5.0*z*z
    return [R3*x,R3*y,R3*z,
      R15*x*y,R15*y*z,0.5*R5*(3.0*z*z-q),R15*x*z,0.5*R15*(x*x-y*y),
      C1*y*(3.0*x*x-y*y),C2*x*y*z,C3*y*(f-q),C4*z*(f-3.0*q),C3*x*(f-q),C5*z*(x*x-y*y),C1*x*(x*x-3.0*y*y)]

def dot(a,b,ca=1,cb=0):
    return lax.dot_general(a,b,(((ca,),(cb,)),((),())),preferred_element_type=F32)

FREE=8
GRP=64; A=8; K=32; E=256

def ld(ref,i,n):
    return jnp.concatenate([ref[h,pl.ds(i,n),:] for h in range(2)],axis=1)

def silu(u):
    return (u+u*jnp.tanh(u)).astype(BF)

def weights(w1_ref,w2_ref,w3_ref,w4_ref,w1b,w2b,w3b,w4p):
    r64=lax.broadcasted_iota(I32,(256,64),0)&63
    pick=jnp.where(r64==lax.broadcasted_iota(I32,(256,64),1),1.0,0.0).astype(BF)
    def spread(w,n):
        v=dot(pick,w,1,1).astype(BF)
        c=lax.broadcasted_iota(I32,(n,4*n),1)&(n-1)
        v=dot(v,jnp.where(c==lax.broadcasted_iota(I32,(n,4*n),0),1.0,0.0).astype(BF))*0.5
        same=(lax.broadcasted_iota(I32,(256,4*n),0)>>6)==(lax.broadcasted_iota(I32,(256,4*n),1)//n)
        return jnp.where(same,v,0.0).astype(BF)
    w1b[...]=spread(w1_ref[...],8)
    w2b[...]=spread(w2_ref[...],64)
    w3b[...]=spread(w3_ref[...],64)
    w4p[...]=jnp.zeros_like(w4p)
    w4p[0,pl.ds(0,64),:]=w4_ref[...]
    w4p[1,pl.ds(64,64),:]=w4_ref[...]


def pipeline(first,n,refs,tables=3):
    tab,lo_s,hi_s,basis_s,y_s,inv_s,w1b,w2b,w3b,w4p,H1,H2,H3,S,W=refs
    iota=lax.broadcasted_iota(I32,(256,E),0).astype(F32).astype(BF)
    ea=lax.broadcasted_iota(I32,(8,E),0)==(lax.broadcasted_iota(I32,(8,E),1)>>5)
    def row(ref,i): return ref[pl.ds(i,1),:]
    def s_amp(t):
        for u in range(4):
            gi=t*4+u
            ys=[jnp.where(ea,ld(y_s,gi*16+m,1),0.0) for m in range(16)]
            ws=W[pl.ds(256*u,256),:]
            r=dot(jnp.concatenate(ys[:4],axis=0).astype(BF),ws[:,:256])
            r2=dot(jnp.concatenate(ys[4:],axis=0).astype(BF),ws[:,256:])
            amps=[r[:8,:128],r[8:,128:],r2[:40,:128],r2[40:,128:]]
            for l in range(4):
                nn=2*l+1
                sq=amps[l]*amps[l]
                tt=sq[:8]
                for m in range(1,nn): tt=tt+sq[8*m:8*m+8]
                o8=gi*8 if isinstance(gi,int) else pl.multiple_of(gi*8,8)
                inv_s[pl.ds(o8,8),pl.ds(128*l,128)]=tt*(1.0/nn)
    def s_rad(t):
        for par in range(2):
            both=jnp.concatenate([H3[:,pl.ds(0,128)],H3[:,pl.ds(128,128)]],axis=0)
            rr=dot(both,w4p[par])
            for half in range(2):
                u=2*half+par; r=rr[256*half:256*half+256]
                ss=S[pl.ds(256*u,256),:].astype(F32)
                for l in range(4):
                    W[pl.ds(256*u,256),pl.ds(128*l,128)]=(r[:,128*l:128*l+128]*ss).astype(BF)
    def pick(hi,cand):
        r=cand[128*(tables-1):]
        for q in range(tables-2,-1,-1): r=jnp.where(hi==float(q),cand[128*q:128*q+128],r)
        return r
    def s_gather(t):
        for u in range(4):
            lo=row(lo_s,t*4+u).astype(BF)
            hi=row(hi_s,t*4+u)
            oh=jnp.where(iota==lo,jnp.ones((),BF),jnp.zeros((),BF))
            cand=dot(tab[pl.ds(0,128*tables),:],oh)
            S[pl.ds(256*u,256),:]=pick(hi,cand).astype(BF).T
    def s_m3(t): H3[...]=silu(dot(w3b[...],H2[...])).T
    def s_m2(t): H2[...]=silu(dot(w2b[...],H1[...]))
    def s_m1(t):
        o=t*32 if isinstance(t,int) else pl.multiple_of(t*32,32)
        H1[...]=silu(dot(w1b[...],ld(basis_s,o,32).astype(BF)))
    stages=[(s_amp,4),(s_rad,3),(s_m3,2),(s_gather,2),(s_m2,1),(s_m1,0)]
    depth=min(4,n)
    def step(t):
        for f,d in stages:
            if isinstance(t,int):
                if 0<=t-d<n: f(t-d+first)
            else: f(t-d+first)
    for t in range(depth): step(t)
    def stepc(t,c): step(t); return c
    lax.fori_loop(depth,n,stepc,0)
    for t in range(n,n+depth): step(t)


def mix(inv_s,wo_ref,spec,emb_ref):
    oht=jnp.where(lax.broadcasted_iota(I32,(emb_ref.shape[0],512),0)==spec,1.0,0.0).astype(BF)
    return (dot(inv_s[...].astype(BF),wo_ref[...])+dot(oht,emb_ref[...],0,0)).astype(BF)


def gather(acc,tl,ll,tiles,table):
    for c in range(3):
        for h in range(2):
            li=ll[:,128*h:128*h+128]; ti=tl[:,128*h:128*h+128]
            for t in tiles:
                v=jnp.take_along_axis(jnp.broadcast_to(table(c,t),li.shape),li,axis=1)
                acc[c][h]=v if acc[c][h] is None else jnp.where(ti==t,v,acc[c][h])
    return acc


def geometry(acc,cen,first,basis_s,y_s):
    n=cen[0].shape[0]
    d=[jnp.concatenate(acc[c],axis=1)-cen[c] for c in range(3)]
    slot=(lax.broadcasted_iota(I32,(n,E),1)&31).astype(F32)
    live=jnp.where(slot<cen[3],1.0,0.0)
    rad=jnp.sqrt(d[0]*d[0]+d[1]*d[1]+d[2]*d[2]+1.0)
    ir=1.0/rad
    def st(ref,at,s,v):
        for h in range(2):
            ref.at[h][pl.ds(first*s+at,n,stride=s),:]=v[:,128*h:128*h+128]
    for k in range(8):
        v=rad-(1.0+0.8*k)
        st(basis_s,k,8,jnp.exp(-0.5*v*v))
    x,y,z=[a*ir for a in d]
    st(y_s,0,16,live)
    for m,v in enumerate(harmonics(x,y,z)):
        st(y_s,m+1,16,v*live)


def per_edge(rows):
    atom=lax.broadcasted_iota(I32,(GRP,512),1)
    g=lax.broadcasted_iota(I32,(GRP,512),0)
    sel=(atom>>3)==g
    M=jnp.concatenate([jnp.where(sel,r,0.0).astype(BF) for r in rows],axis=0)
    er=lax.broadcasted_iota(I32,(512,E),0)&7
    ec=lax.broadcasted_iota(I32,(512,E),1)>>5
    return dot(M,jnp.where(er==ec,1.0,0.0).astype(BF))


def whole(ins,out_ref,bufs,scratch):
    sem,tab,nb_s,lo_s,hi_s,basis_s,y_s,inv_s,w1b,w2b,w3b,w4p,H1,H2,H3,S,W=scratch
    feats, pos, cnt, nbr, spec, gfeat, wn, w1, w2, w3, w4, wo, emb = ins
    (extf_ref, own_ref, cnt_ref, nbr_ref, spec_ref, gpos_ref, wn_ref, w1_ref, w2_ref, w3_ref, w4_ref, wo_ref, emb_ref) = bufs
    pairs = [(feats, extf_ref.at[pl.ds(64, 512), :]), (pos, own_ref), (cnt, cnt_ref), (nbr, nbr_ref), (spec, spec_ref)]
    for q, start in enumerate((0, 576, 640, 704)):
        pairs.append((gfeat.at[q, pl.ds(0, 64), :], extf_ref.at[pl.ds(start, 64), :]))
        pairs.append((gfeat.at[q, pl.ds(64, 16), :], gpos_ref.at[q]))
    pairs += [(wn, wn_ref), (w1, w1_ref), (w2, w2_ref), (w3, w3_ref), (w4, w4_ref), (wo, wo_ref), (emb, emb_ref)]
    cps = [pltpu.make_async_copy(x, y, sem.at[i]) for i, (x, y) in enumerate(pairs)]
    for c in cps:
        c.start()
    for c in cps:
        c.wait()
    wn=wn_ref[...]
    for t in range(3):
        tab[pl.ds(128*t,128),:]=dot(wn,extf_ref[pl.ds(256*t,256),:],0,1).astype(BF)
    weights(w1_ref,w2_ref,w3_ref,w4_ref,w1b,w2b,w3b,w4p)
    nb_s[:,pl.ds(0,32)]=nbr_ref[...].T
    idx=jnp.concatenate([nb_s[pl.ds(a,GRP,stride=A),:][:,:32] for a in range(A)],axis=1)
    lo_s[...]=(idx&255).astype(F32)
    hi_s[...]=(idx>>8).astype(F32)
    own=own_ref[...].astype(F32)
    cen=per_edge([own[0:1],own[1:2],own[2:3],cnt_ref[...].astype(F32)])
    gp=[gpos_ref[q,pl.ds(0,3),:].astype(F32)[:,:64] for q in range(4)]
    ext=jnp.concatenate([gp[0],own,gp[1],gp[2],gp[3]],axis=1)
    sh=jnp.where(lax.broadcasted_iota(I32,(1,128),1)<64,-4.0,4.0)
    acc=gather([[None,None] for _ in range(3)],idx>>7,idx&127,range(6),lambda c,t: ext[c:c+1,128*t:128*t+128]+(sh if c==0 and t==5 else 0.0))
    geometry(acc,[cen[64*c:64*c+64] for c in range(4)],0,basis_s,y_s)
    pipeline(0,GRP//4,(tab,lo_s,hi_s,basis_s,y_s,inv_s,w1b,w2b,w3b,w4p,H1,H2,H3,S,W))
    out_ref[...]=mix(inv_s,wo_ref,spec_ref[...],emb_ref)


def body(*refs,n_in):
    ins=refs[:n_in]; out_ref,recv,nf_ref=refs[n_in:n_in+3]; bufs=refs[n_in+3:2*n_in+3]
    (send,perm,sem,ssem,rsem,tab,nb_s,lo_s,hi_s,basis_s,y_s,inv_s,w1b,w2b,w3b,w4p,H1,H2,H3,S,W)=refs[2*n_in+3:]
    d=lax.axis_index("dom"); j=lax.axis_index("ch")
    nd=lax.axis_size("dom"); nc=lax.axis_size("ch")
    up={"dom":lax.rem(d+1,nd)}; down={"dom":lax.rem(d+nd-1,nd)}
    nxt={"ch":lax.rem(j+1,nc)}; prv={"ch":lax.rem(j+nc-1,nc)}
    barrier=pltpu.get_barrier_semaphore()
    for to in (up,down,nxt,prv):
        pl.semaphore_signal(barrier,inc=1,device_id=to,device_id_type=MESH)
    cps=[pltpu.make_async_copy(x,y,sem.at[i]) for i,(x,y) in enumerate(zip(ins,bufs))]
    for c in cps: c.start()
    f_ref,own_ref,gid_ref,cnt_ref,nbr_ref,spec_ref,wn_ref,w1_ref,w2_ref,w3_ref,w4_ref,wo_ref,emb_ref=bufs
    for c in cps[:3]: c.wait()
    at=lax.broadcasted_iota(I32,(512,128),0)
    ln=lax.broadcasted_iota(I32,(512,128),1)
    pad=jnp.full((1,64),-1,I32)
    g0=jnp.concatenate([gid_ref[pl.ds(0,1),:],pad],axis=1)
    g1=jnp.concatenate([gid_ref[pl.ds(1,1),:],pad],axis=1)
    p16=jnp.concatenate([own_ref[...].astype(F32),jnp.zeros((13,512),F32)],axis=0).astype(BF)
    f=f_ref[...]
    sels=[(at==ln+448),(at==ln)&(ln<64),at==g0,at==g1]
    for q in range(4):
        sl=jnp.where(sels[q],1.0,0.0).astype(BF)
        send[q,pl.ds(64,16),:]=dot(p16,sl).astype(BF)
        if q==0: send[q,pl.ds(0,64),:]=f[448:]
        elif q==1: send[q,pl.ds(0,64),:]=f[:64]
        else: send[q,pl.ds(0,64),:]=dot(sl[:,:64],f,0,0).astype(BF)
    for c in cps[3:]: c.wait()
    wn=wn_ref[...]
    def table(t,x): tab[pl.ds(128*t,128),:]=dot(wn,x,0,1).astype(BF)
    table(0,f[:256]); table(1,f[256:])
    nb=nbr_ref[...]-64
    nb=jnp.where(nb<0,nb+768,nb)
    cnt=cnt_ref[...]
    far=(nb>=512)&(lax.broadcasted_iota(I32,(K,512),0)<cnt)
    free=1.0-jnp.max(jnp.where(far,1.0,0.0),axis=0,keepdims=True)
    ra=lax.broadcasted_iota(I32,(512,512),0)
    ca=lax.broadcasted_iota(I32,(512,512),1)
    below=jnp.where(ra<ca,1.0,0.0).astype(BF)
    before=dot(jnp.broadcast_to(free,(8,512)).astype(BF),below)[0:1]
    total=jnp.sum(free,axis=1,keepdims=True)
    nf_ref[...]=jnp.broadcast_to(total,(8,128))
    place=jnp.where(free>0.5,before,total+ca[0:1].astype(F32)-before)
    pm=jnp.where(ra==place.astype(I32),1.0,0.0).astype(BF)
    perm[...]=pm.T
    own=own_ref[...].astype(F32)
    R=jnp.concatenate([(nb&255).astype(F32),(nb>>8).astype(F32),own,cnt.astype(F32),spec_ref[...].astype(F32),jnp.zeros((59,512),F32)],axis=0).astype(BF)
    moved=dot(pm,R,1,1)
    nb_s[...]=moved
    atoms=moved.T[64:72]
    parts=[nb_s[pl.ds(a,GRP,stride=A),:] for a in range(A)]
    lo=jnp.concatenate([p[:,:32] for p in parts],axis=1)
    hi=jnp.concatenate([p[:,32:64] for p in parts],axis=1)
    lo_s[...]=lo
    hi_s[...]=hi
    lo=lo.astype(I32)
    tl=hi.astype(I32)*2+(lo>>7); ll=lo&127
    cen=per_edge([atoms[q:q+1] for q in range(4)])
    weights(w1_ref,w2_ref,w3_ref,w4_ref,w1b,w2b,w3b,w4p)
    G=4*FREE
    inner=lambda c,t: own[c:c+1,128*t:128*t+128]
    pl.semaphore_wait(barrier,4)
    def copy(q,slot,to):
        return pltpu.make_async_remote_copy(src_ref=send.at[q],dst_ref=recv.at[slot],send_sem=ssem.at[q],recv_sem=rsem.at[slot],device_id=to,device_id_type=MESH)
    rc=[copy(2,3,down),copy(3,2,up),copy(0,0,nxt),copy(1,1,prv)]
    for c in rc: c.start()

    acc=gather([[None,None] for _ in range(3)],tl[:G],ll[:G],range(4),inner)
    geometry(acc,[cen[64*c:64*c+G] for c in range(4)],0,basis_s,y_s)
    work=(tab,lo_s,hi_s,basis_s,y_s,inv_s,w1b,w2b,w3b,w4p,H1,H2,H3,S,W)
    pipeline(0,FREE,work,2)
    acc=gather([[None,None] for _ in range(3)],tl[G:],ll[G:],range(4),inner)
    for c in rc: c.wait()
    @pl.when(j==0)
    def _(): recv[0]=jnp.zeros((80,128),BF)
    @pl.when(j==nc-1)
    def _(): recv[1]=jnp.zeros((80,128),BF)
    table(2,jnp.concatenate([recv[q,pl.ds(0,64),:] for q in (1,2,3,0)],axis=0))
    gp=[recv[q,pl.ds(64,16),:].astype(F32)[:3,:64] for q in (1,2,3,0)]
    outer=[[jnp.concatenate([gp[0][c:c+1],gp[1][c:c+1]-(4.0 if c==0 else 0.0)],axis=1),jnp.concatenate([gp[2][c:c+1]+(4.0 if c==0 else 0.0),gp[3][c:c+1]],axis=1)] for c in range(3)]
    acc=gather(acc,tl[G:],ll[G:],(4,5),lambda c,t: outer[c][t-4])
    geometry(acc,[cen[64*c+G:64*c+64] for c in range(4)],G,basis_s,y_s)
    pipeline(FREE,GRP//4-FREE,work)
    res=mix(inv_s,wo_ref,atoms[4:5].astype(I32),emb_ref)
    out_ref[...]=dot(perm[...],res).astype(BF)


def finish_body(*refs,n_in):
    done,nf=refs[:2]; ins=refs[2:n_in]; out=refs[n_in]
    nfb,sems=refs[n_in+1:n_in+3]; bufs=refs[n_in+3:2*n_in+1]; scratch=refs[2*n_in+1:]
    one=pltpu.make_async_copy(nf,nfb,sems.at[0])
    two=pltpu.make_async_copy(done,out,sems.at[1])
    one.start(); two.start()
    one.wait(); two.wait()
    @pl.when(jnp.max(nfb[...])<32.0*FREE)
    def _(): whole(ins,out,bufs,scratch)


def block(node_feats,positions,species,neighbours,counts,ghost_ids,w_node,w_r1,w_r2,w_r3,w_r4,w_out,species_emb):
    V=pltpu.VMEM
    common=[V((384,256),BF),V((512,128),F32),V((64,256),F32),V((64,256),F32),V((2,512,128),F32),V((2,1024,128),F32),V((512,512),F32),
          V((256,32),BF),V((256,256),BF),V((256,256),BF),V((2,128,512),BF),V((256,256),BF),V((256,256),BF),V((256,256),BF),V((1024,128),BF),V((1024,512),BF)]
    counts=counts.reshape(1,-1); species=species.reshape(1,-1); neighbours=neighbours.T
    ws=(w_node,w_r1,w_r2,w_r3,w_r4,w_out,species_emb)
    args=(node_feats,positions,ghost_ids,counts,neighbours,species)+ws
    n_in=len(args)
    done,ghosts,free=pl.pallas_call(functools.partial(body,n_in=n_in),
        out_shape=[jax.ShapeDtypeStruct((512,128),BF),jax.ShapeDtypeStruct((4,80,128),BF),jax.ShapeDtypeStruct((8,128),F32)],
        in_specs=[pl.BlockSpec(memory_space=pl.ANY)]*n_in,
        out_specs=[pl.BlockSpec(memory_space=pltpu.VMEM)]*3,
        scratch_shapes=[V(x.shape,x.dtype) for x in args]+[V((4,80,128),BF),V((512,512),BF),
          pltpu.SemaphoreType.DMA((n_in,)),pltpu.SemaphoreType.DMA((4,)),pltpu.SemaphoreType.DMA((4,)),V((384,256),BF),V((512,128),F32),V((64,256),F32),V((64,256),F32),V((2,512,128),F32),V((2,1024,128),F32),V((512,512),F32),
          V((256,32),BF),V((256,256),BF),V((256,256),BF),V((2,128,512),BF),V((256,256),BF),V((256,256),BF),V((256,256),BF),V((1024,128),BF),V((1024,512),BF)],
        compiler_params=pltpu.CompilerParams(collective_id=0,has_side_effects=True,vmem_limit_bytes=60*2**20),
        )(*args)
    args=(done,free,node_feats,positions,counts,neighbours,species,ghosts)+ws
    n_in=len(args)
    bufs=[V((768,128),BF)]+[V(x.shape,x.dtype) for x in args[3:7]]+[V((4,16,128),BF)]+[V(x.shape,x.dtype) for x in ws]
    return pl.pallas_call(functools.partial(finish_body,n_in=n_in),
        out_shape=jax.ShapeDtypeStruct((512,128),BF),
        in_specs=[pl.BlockSpec(memory_space=pl.ANY)]*n_in,
        out_specs=pl.BlockSpec(memory_space=pltpu.VMEM),
        scratch_shapes=[V((8,128),F32),pltpu.SemaphoreType.DMA((2,))]+bufs+[pltpu.SemaphoreType.DMA((20,)),V((384,256),BF),V((512,128),I32),V((64,256),F32),V((64,256),F32),V((2,512,128),F32),V((2,1024,128),F32),V((512,512),F32),
          V((256,32),BF),V((256,256),BF),V((256,256),BF),V((2,128,512),BF),V((256,256),BF),V((256,256),BF),V((256,256),BF),V((1024,128),BF),V((1024,512),BF)],
        compiler_params=pltpu.CompilerParams(vmem_limit_bytes=60*2**20),
        )(*args)


def solution(mesh):
    each=P(("dom","ch"),None)
    flat=P(("dom","ch"))
    cols=P(None,("dom","ch"))
    return jax.shard_map(block,mesh=mesh,
        in_specs=(each,cols,flat,each,flat,cols)+(P(),)*7,
        out_specs=each,check_vma=False)
```

```python
import functools
import math

import jax
import jax.numpy as jnp
from jax import lax
from jax.experimental import pallas as pl
from jax.experimental.pallas import tpu as pltpu
from jax.sharding import PartitionSpec as P

F32 = jnp.float32
BF = jnp.bfloat16
I32 = jnp.int32
MESH = pl.DeviceIdType.MESH
R3=math.sqrt(3.0);R5=math.sqrt(5.0);R15=math.sqrt(15.0)
C1=0.5*math.sqrt(17.5);C2=math.sqrt(105.0);C3=0.5*math.sqrt(10.5);C4=0.5*math.sqrt(7.0);C5=0.5*math.sqrt(105.0)

def harmonics(x,y,z):
    q=x*x+y*y+z*z
    f=5.0*z*z
    return [R3*x,R3*y,R3*z,
      R15*x*y,R15*y*z,0.5*R5*(3.0*z*z-q),R15*x*z,0.5*R15*(x*x-y*y),
      C1*y*(3.0*x*x-y*y),C2*x*y*z,C3*y*(f-q),C4*z*(f-3.0*q),C3*x*(f-q),C5*z*(x*x-y*y),C1*x*(x*x-3.0*y*y)]

def dot(a,b,ca=1,cb=0):
    return lax.dot_general(a,b,(((ca,),(cb,)),((),())),preferred_element_type=F32)

FREE=8
GRP=64; A=8; K=32; E=256

def ld(ref,i,n):
    return jnp.concatenate([ref[h,pl.ds(i,n),:] for h in range(2)],axis=1)

def silu(u):
    return (u+u*jnp.tanh(u)).astype(BF)

def weights(w1_ref,w2_ref,w3_ref,w4_ref,w1b,w2b,w3b,w4p):
    r64=lax.broadcasted_iota(I32,(256,64),0)&63
    pick=jnp.where(r64==lax.broadcasted_iota(I32,(256,64),1),1.0,0.0).astype(BF)
    def spread(w,n):
        v=dot(pick,w,1,1).astype(BF)
        c=lax.broadcasted_iota(I32,(n,4*n),1)&(n-1)
        v=dot(v,jnp.where(c==lax.broadcasted_iota(I32,(n,4*n),0),1.0,0.0).astype(BF))*0.5
        same=(lax.broadcasted_iota(I32,(256,4*n),0)>>6)==(lax.broadcasted_iota(I32,(256,4*n),1)//n)
        return jnp.where(same,v,0.0).astype(BF)
    w1b[...]=spread(w1_ref[...],8)
    w2b[...]=spread(w2_ref[...],64)
    w3b[...]=spread(w3_ref[...],64)
    w4p[...]=jnp.zeros_like(w4p)
    w4p[0,pl.ds(0,64),:]=w4_ref[...]
    w4p[1,pl.ds(64,64),:]=w4_ref[...]


def pipeline(first,n,refs,tables=3,hook=None):
    tab,lo_s,hi_s,basis_s,y_s,inv_s,w1b,w2b,w3b,w4p,H1,H2,H3,S,W=refs
    iota=lax.broadcasted_iota(I32,(256,E),0).astype(F32).astype(BF)
    ea=lax.broadcasted_iota(I32,(8,E),0)==(lax.broadcasted_iota(I32,(8,E),1)>>5)
    def row(ref,i): return ref[pl.ds(i,1),:]
    def s_amp(t):
        for u in range(4):
            gi=t*4+u
            ys=[jnp.where(ea,ld(y_s,gi*16+m,1),0.0) for m in range(16)]
            ws=W[pl.ds(256*u,256),:]
            r=dot(jnp.concatenate(ys[:4],axis=0).astype(BF),ws[:,:256])
            r2=dot(jnp.concatenate(ys[4:],axis=0).astype(BF),ws[:,256:])
            amps=[r[:8,:128],r[8:,128:],r2[:40,:128],r2[40:,128:]]
            for l in range(4):
                nn=2*l+1
                sq=amps[l]*amps[l]
                tt=sq[:8]
                for m in range(1,nn): tt=tt+sq[8*m:8*m+8]
                o8=gi*8 if isinstance(gi,int) else pl.multiple_of(gi*8,8)
                inv_s[pl.ds(o8,8),pl.ds(128*l,128)]=tt*(1.0/nn)
    def s_rad(t):
        for par in range(2):
            both=jnp.concatenate([H3[:,pl.ds(0,128)],H3[:,pl.ds(128,128)]],axis=0)
            rr=dot(both,w4p[par])
            for half in range(2):
                u=2*half+par; r=rr[256*half:256*half+256]
                ss=S[pl.ds(256*u,256),:].astype(F32)
                for l in range(4):
                    W[pl.ds(256*u,256),pl.ds(128*l,128)]=(r[:,128*l:128*l+128]*ss).astype(BF)
    def pick(hi,cand):
        r=cand[128*(tables-1):]
        for q in range(tables-2,-1,-1): r=jnp.where(hi==float(q),cand[128*q:128*q+128],r)
        return r
    def s_gather(t):
        for u in range(4):
            lo=row(lo_s,t*4+u).astype(BF)
            hi=row(hi_s,t*4+u)
            oh=jnp.where(iota==lo,jnp.ones((),BF),jnp.zeros((),BF))
            cand=dot(tab[pl.ds(0,128*tables),:],oh)
            S[pl.ds(256*u,256),:]=pick(hi,cand).astype(BF).T
    def s_m3(t): H3[...]=silu(dot(w3b[...],H2[...])).T
    def s_m2(t): H2[...]=silu(dot(w2b[...],H1[...]))
    def s_m1(t):
        o=t*32 if isinstance(t,int) else pl.multiple_of(t*32,32)
        H1[...]=silu(dot(w1b[...],ld(basis_s,o,32).astype(BF)))
    stages=[(s_amp,4),(s_rad,3),(s_m3,2),(s_gather,2),(s_m2,1),(s_m1,0)]
    depth=min(4,n)
    def step(t):
        for f,d in stages:
            if isinstance(t,int):
                if 0<=t-d<n: f(t-d+first)
            else: f(t-d+first)
    for t in range(depth):
        if t==2 and hook is not None: hook()
        step(t)
    def stepc(t,c): step(t); return c
    lax.fori_loop(depth,n,stepc,0)
    for t in range(n,n+depth): step(t)


def mix(inv_s,wo_ref,spec,emb_ref):
    oht=jnp.where(lax.broadcasted_iota(I32,(emb_ref.shape[0],512),0)==spec,1.0,0.0).astype(BF)
    return (dot(inv_s[...].astype(BF),wo_ref[...])+dot(oht,emb_ref[...],0,0)).astype(BF)


def gather(acc,tl,ll,tiles,table):
    for c in range(3):
        for h in range(2):
            li=ll[:,128*h:128*h+128]; ti=tl[:,128*h:128*h+128]
            for t in tiles:
                v=jnp.take_along_axis(jnp.broadcast_to(table(c,t),li.shape),li,axis=1)
                acc[c][h]=v if acc[c][h] is None else jnp.where(ti==t,v,acc[c][h])
    return acc


def geometry(acc,cen,first,basis_s,y_s):
    n=cen[0].shape[0]
    d=[jnp.concatenate(acc[c],axis=1)-cen[c] for c in range(3)]
    slot=(lax.broadcasted_iota(I32,(n,E),1)&31).astype(F32)
    live=jnp.where(slot<cen[3],1.0,0.0)
    rad=jnp.sqrt(d[0]*d[0]+d[1]*d[1]+d[2]*d[2]+1.0)
    ir=1.0/rad
    def st(ref,at,s,v):
        for h in range(2):
            ref.at[h][pl.ds(first*s+at,n,stride=s),:]=v[:,128*h:128*h+128]
    for k in range(8):
        v=rad-(1.0+0.8*k)
        st(basis_s,k,8,jnp.exp(-0.5*v*v))
    x,y,z=[a*ir for a in d]
    st(y_s,0,16,live)
    for m,v in enumerate(harmonics(x,y,z)):
        st(y_s,m+1,16,v*live)


def per_edge(rows):
    atom=lax.broadcasted_iota(I32,(GRP,512),1)
    g=lax.broadcasted_iota(I32,(GRP,512),0)
    sel=(atom>>3)==g
    M=jnp.concatenate([jnp.where(sel,r,0.0).astype(BF) for r in rows],axis=0)
    er=lax.broadcasted_iota(I32,(512,E),0)&7
    ec=lax.broadcasted_iota(I32,(512,E),1)>>5
    return dot(M,jnp.where(er==ec,1.0,0.0).astype(BF))


def whole(ins,out_ref,bufs,scratch):
    sem,tab,nb_s,lo_s,hi_s,basis_s,y_s,inv_s,w1b,w2b,w3b,w4p,H1,H2,H3,S,W=scratch
    feats, pos, cnt, nbr, spec, gfeat, wn, w1, w2, w3, w4, wo, emb = ins
    (extf_ref, own_ref, cnt_ref, nbr_ref, spec_ref, gpos_ref, wn_ref, w1_ref, w2_ref, w3_ref, w4_ref, wo_ref, emb_ref) = bufs
    pairs = [(feats, extf_ref.at[pl.ds(64, 512), :]), (pos, own_ref), (cnt, cnt_ref), (nbr, nbr_ref), (spec, spec_ref)]
    for q, start in enumerate((0, 576, 640, 704)):
        pairs.append((gfeat.at[q, pl.ds(0, 64), :], extf_ref.at[pl.ds(start, 64), :]))
        pairs.append((gfeat.at[q, pl.ds(64, 16), :], gpos_ref.at[q]))
    pairs += [(wn, wn_ref), (w1, w1_ref), (w2, w2_ref), (w3, w3_ref), (w4, w4_ref), (wo, wo_ref), (emb, emb_ref)]
    cps = [pltpu.make_async_copy(x, y, sem.at[i]) for i, (x, y) in enumerate(pairs)]
    for c in cps:
        c.start()
    for c in cps:
        c.wait()
    wn=wn_ref[...]
    for t in range(3):
        tab[pl.ds(128*t,128),:]=dot(wn,extf_ref[pl.ds(256*t,256),:],0,1).astype(BF)
    weights(w1_ref,w2_ref,w3_ref,w4_ref,w1b,w2b,w3b,w4p)
    nb_s[:,pl.ds(0,32)]=nbr_ref[...].T
    idx=jnp.concatenate([nb_s[pl.ds(a,GRP,stride=A),:][:,:32] for a in range(A)],axis=1)
    lo_s[...]=(idx&255).astype(F32)
    hi_s[...]=(idx>>8).astype(F32)
    own=own_ref[...].astype(F32)
    cen=per_edge([own[0:1],own[1:2],own[2:3],cnt_ref[...].astype(F32)])
    gp=[gpos_ref[q,pl.ds(0,3),:].astype(F32)[:,:64] for q in range(4)]
    ext=jnp.concatenate([gp[0],own,gp[1],gp[2],gp[3]],axis=1)
    sh=jnp.where(lax.broadcasted_iota(I32,(1,128),1)<64,-4.0,4.0)
    acc=gather([[None,None] for _ in range(3)],idx>>7,idx&127,range(6),lambda c,t: ext[c:c+1,128*t:128*t+128]+(sh if c==0 and t==5 else 0.0))
    geometry(acc,[cen[64*c:64*c+64] for c in range(4)],0,basis_s,y_s)
    pipeline(0,GRP//4,(tab,lo_s,hi_s,basis_s,y_s,inv_s,w1b,w2b,w3b,w4p,H1,H2,H3,S,W))
    out_ref[...]=mix(inv_s,wo_ref,spec_ref[...],emb_ref)


def body(*refs,n_in):
    ins=refs[:n_in]; out_ref,recv,nf_ref=refs[n_in:n_in+3]; bufs=refs[n_in+3:2*n_in+3]
    (send,perm,held,sem,ssem,rsem,tab,nb_s,lo_s,hi_s,basis_s,y_s,inv_s,w1b,w2b,w3b,w4p,H1,H2,H3,S,W)=refs[2*n_in+3:]
    d=lax.axis_index("dom"); j=lax.axis_index("ch")
    nd=lax.axis_size("dom"); nc=lax.axis_size("ch")
    up={"dom":lax.rem(d+1,nd)}; down={"dom":lax.rem(d+nd-1,nd)}
    nxt={"ch":lax.rem(j+1,nc)}; prv={"ch":lax.rem(j+nc-1,nc)}
    barrier=pltpu.get_barrier_semaphore()
    for to in (up,down,nxt,prv):
        pl.semaphore_signal(barrier,inc=1,device_id=to,device_id_type=MESH)
    cps=[pltpu.make_async_copy(x,y,sem.at[i]) for i,(x,y) in enumerate(zip(ins,bufs))]
    for c in cps: c.start()
    f_ref,own_ref,gid_ref,cnt_ref,nbr_ref,spec_ref,wn_ref,w1_ref,w2_ref,w3_ref,w4_ref,wo_ref,emb_ref=bufs
    for c in cps[:3]: c.wait()
    at=lax.broadcasted_iota(I32,(512,128),0)
    ln=lax.broadcasted_iota(I32,(512,128),1)
    pad=jnp.full((1,64),-1,I32)
    g0=jnp.concatenate([gid_ref[pl.ds(0,1),:],pad],axis=1)
    g1=jnp.concatenate([gid_ref[pl.ds(1,1),:],pad],axis=1)
    p16=jnp.concatenate([own_ref[...].astype(F32),jnp.zeros((13,512),F32)],axis=0).astype(BF)
    f=f_ref[...]
    sels=[(at==ln+448),(at==ln)&(ln<64),at==g0,at==g1]
    for q in range(4):
        sl=jnp.where(sels[q],1.0,0.0).astype(BF)
        send[q,pl.ds(64,16),:]=dot(p16,sl).astype(BF)
        if q==0: send[q,pl.ds(0,64),:]=f[448:]
        elif q==1: send[q,pl.ds(0,64),:]=f[:64]
        else: send[q,pl.ds(0,64),:]=dot(sl[:,:64],f,0,0).astype(BF)
    for c in cps[3:]: c.wait()
    wn=wn_ref[...]
    def table(t,x): tab[pl.ds(128*t,128),:]=dot(wn,x,0,1).astype(BF)
    table(0,f[:256]); table(1,f[256:])
    nb=nbr_ref[...]-64
    nb=jnp.where(nb<0,nb+768,nb)
    cnt=cnt_ref[...]
    far=(nb>=512)&(lax.broadcasted_iota(I32,(K,512),0)<cnt)
    free=1.0-jnp.max(jnp.where(far,1.0,0.0),axis=0,keepdims=True)
    ra=lax.broadcasted_iota(I32,(512,512),0)
    ca=lax.broadcasted_iota(I32,(512,512),1)
    below=jnp.where(ra<ca,1.0,0.0).astype(BF)
    before=dot(jnp.broadcast_to(free,(8,512)).astype(BF),below)[0:1]
    total=jnp.sum(free,axis=1,keepdims=True)
    nf_ref[...]=jnp.broadcast_to(total,(8,128))
    place=jnp.where(free>0.5,before,total+ca[0:1].astype(F32)-before)
    pm=jnp.where(ra==place.astype(I32),1.0,0.0).astype(BF)
    perm[...]=pm.T
    own=own_ref[...].astype(F32)
    R=jnp.concatenate([(nb&255).astype(F32),(nb>>8).astype(F32),own,cnt.astype(F32),spec_ref[...].astype(F32),jnp.zeros((59,512),F32)],axis=0).astype(BF)
    moved=dot(pm,R,1,1)
    nb_s[...]=moved
    atoms=moved.T[64:72]
    parts=[nb_s[pl.ds(a,GRP,stride=A),:] for a in range(A)]
    lo=jnp.concatenate([p[:,:32] for p in parts],axis=1)
    hi=jnp.concatenate([p[:,32:64] for p in parts],axis=1)
    lo_s[...]=lo
    hi_s[...]=hi
    lo=lo.astype(I32)
    tl=hi.astype(I32)*2+(lo>>7); ll=lo&127
    cen=per_edge([atoms[q:q+1] for q in range(4)])
    weights(w1_ref,w2_ref,w3_ref,w4_ref,w1b,w2b,w3b,w4p)
    G=4*FREE
    inner=lambda c,t: own[c:c+1,128*t:128*t+128]
    def copy(q,slot,to):
        return pltpu.make_async_remote_copy(src_ref=send.at[q],dst_ref=recv.at[slot],send_sem=ssem.at[q],recv_sem=rsem.at[slot],device_id=to,device_id_type=MESH)
    rc=[copy(2,3,down),copy(3,2,up),copy(0,0,nxt),copy(1,1,prv)]
    def send_all():
        pl.semaphore_wait(barrier,4)
        for c in rc: c.start()

    acc=gather([[None,None] for _ in range(3)],tl[:G],ll[:G],range(4),inner)
    geometry(acc,[cen[64*c:64*c+G] for c in range(4)],0,basis_s,y_s)
    work=(tab,lo_s,hi_s,basis_s,y_s,inv_s,w1b,w2b,w3b,w4p,H1,H2,H3,S,W)
    later=gather([[None,None] for _ in range(3)],tl[G:],ll[G:],range(4),inner)
    for c in range(3):
        for h in range(2): held[c,h]=later[c][h]
    pipeline(0,FREE,work,2,send_all)
    for c in rc: c.wait()
    @pl.when(j==0)
    def _(): recv[0]=jnp.zeros((80,128),BF)
    @pl.when(j==nc-1)
    def _(): recv[1]=jnp.zeros((80,128),BF)
    table(2,jnp.concatenate([recv[q,pl.ds(0,64),:] for q in (1,2,3,0)],axis=0))
    gp=[recv[q,pl.ds(64,16),:].astype(F32)[:3,:64] for q in (1,2,3,0)]
    outer=[[jnp.concatenate([gp[0][c:c+1],gp[1][c:c+1]-(4.0 if c==0 else 0.0)],axis=1),jnp.concatenate([gp[2][c:c+1]+(4.0 if c==0 else 0.0),gp[3][c:c+1]],axis=1)] for c in range(3)]
    acc=gather([[held[c,h] for h in range(2)] for c in range(3)],tl[G:],ll[G:],(4,5),lambda c,t: outer[c][t-4])
    geometry(acc,[cen[64*c+G:64*c+64] for c in range(4)],G,basis_s,y_s)
    pipeline(FREE,GRP//4-FREE,work)
    res=mix(inv_s,wo_ref,atoms[4:5].astype(I32),emb_ref)
    out_ref[...]=dot(perm[...],res).astype(BF)


def finish_body(*refs,n_in):
    done,nf=refs[:2]; ins=refs[2:n_in]; out=refs[n_in]
    nfb,sems=refs[n_in+1:n_in+3]; bufs=refs[n_in+3:2*n_in+1]; scratch=refs[2*n_in+1:]
    one=pltpu.make_async_copy(nf,nfb,sems.at[0])
    two=pltpu.make_async_copy(done,out,sems.at[1])
    one.start(); two.start()
    one.wait(); two.wait()
    @pl.when(jnp.max(nfb[...])<32.0*FREE)
    def _(): whole(ins,out,bufs,scratch)


def block(node_feats,positions,species,neighbours,counts,ghost_ids,w_node,w_r1,w_r2,w_r3,w_r4,w_out,species_emb):
    V=pltpu.VMEM
    common=[V((384,256),BF),V((512,128),F32),V((64,256),F32),V((64,256),F32),V((2,512,128),F32),V((2,1024,128),F32),V((512,512),F32),
          V((256,32),BF),V((256,256),BF),V((256,256),BF),V((2,128,512),BF),V((256,256),BF),V((256,256),BF),V((256,256),BF),V((1024,128),BF),V((1024,512),BF)]
    counts=counts.reshape(1,-1); species=species.reshape(1,-1); neighbours=neighbours.T
    ws=(w_node,w_r1,w_r2,w_r3,w_r4,w_out,species_emb)
    args=(node_feats,positions,ghost_ids,counts,neighbours,species)+ws
    n_in=len(args)
    done,ghosts,free=pl.pallas_call(functools.partial(body,n_in=n_in),
        out_shape=[jax.ShapeDtypeStruct((512,128),BF),jax.ShapeDtypeStruct((4,80,128),BF),jax.ShapeDtypeStruct((8,128),F32)],
        in_specs=[pl.BlockSpec(memory_space=pl.ANY)]*n_in,
        out_specs=[pl.BlockSpec(memory_space=pltpu.VMEM)]*3,
        scratch_shapes=[V(x.shape,x.dtype) for x in args]+[V((4,80,128),BF),V((512,512),BF),V((3,2,GRP-4*FREE,128),F32),
          pltpu.SemaphoreType.DMA((n_in,)),pltpu.SemaphoreType.DMA((4,)),pltpu.SemaphoreType.DMA((4,)),V((384,256),BF),V((512,128),F32),V((64,256),F32),V((64,256),F32),V((2,512,128),F32),V((2,1024,128),F32),V((512,512),F32),
          V((256,32),BF),V((256,256),BF),V((256,256),BF),V((2,128,512),BF),V((256,256),BF),V((256,256),BF),V((256,256),BF),V((1024,128),BF),V((1024,512),BF)],
        compiler_params=pltpu.CompilerParams(collective_id=0,has_side_effects=True,vmem_limit_bytes=60*2**20),
        )(*args)
    args=(done,free,node_feats,positions,counts,neighbours,species,ghosts)+ws
    n_in=len(args)
    bufs=[V((768,128),BF)]+[V(x.shape,x.dtype) for x in args[3:7]]+[V((4,16,128),BF)]+[V(x.shape,x.dtype) for x in ws]
    return pl.pallas_call(functools.partial(finish_body,n_in=n_in),
        out_shape=jax.ShapeDtypeStruct((512,128),BF),
        in_specs=[pl.BlockSpec(memory_space=pl.ANY)]*n_in,
        out_specs=pl.BlockSpec(memory_space=pltpu.VMEM),
        scratch_shapes=[V((8,128),F32),pltpu.SemaphoreType.DMA((2,))]+bufs+[pltpu.SemaphoreType.DMA((20,)),V((384,256),BF),V((512,128),I32),V((64,256),F32),V((64,256),F32),V((2,512,128),F32),V((2,1024,128),F32),V((512,512),F32),
          V((256,32),BF),V((256,256),BF),V((256,256),BF),V((2,128,512),BF),V((256,256),BF),V((256,256),BF),V((256,256),BF),V((1024,128),BF),V((1024,512),BF)],
        compiler_params=pltpu.CompilerParams(vmem_limit_bytes=60*2**20),
        )(*args)


def solution(mesh):
    each=P(("dom","ch"),None)
    flat=P(("dom","ch"))
    cols=P(None,("dom","ch"))
    return jax.shard_map(block,mesh=mesh,
        in_specs=(each,cols,flat,each,flat,cols)+(P(),)*7,
        out_specs=each,check_vma=False)
```

```python
import functools
import math

import jax
import jax.numpy as jnp
from jax import lax
from jax.experimental import pallas as pl
from jax.experimental.pallas import tpu as pltpu
from jax.sharding import PartitionSpec as P

F32 = jnp.float32
BF = jnp.bfloat16
I32 = jnp.int32
MESH = pl.DeviceIdType.MESH
R3=math.sqrt(3.0);R5=math.sqrt(5.0);R15=math.sqrt(15.0)
C1=0.5*math.sqrt(17.5);C2=math.sqrt(105.0);C3=0.5*math.sqrt(10.5);C4=0.5*math.sqrt(7.0);C5=0.5*math.sqrt(105.0)

def harmonics(x,y,z):
    q=x*x+y*y+z*z
    f=5.0*z*z
    return [R3*x,R3*y,R3*z,
      R15*x*y,R15*y*z,0.5*R5*(3.0*z*z-q),R15*x*z,0.5*R15*(x*x-y*y),
      C1*y*(3.0*x*x-y*y),C2*x*y*z,C3*y*(f-q),C4*z*(f-3.0*q),C3*x*(f-q),C5*z*(x*x-y*y),C1*x*(x*x-3.0*y*y)]

def dot(a,b,ca=1,cb=0):
    return lax.dot_general(a,b,(((ca,),(cb,)),((),())),preferred_element_type=F32)

FREE=8
GRP=64; A=8; K=32; E=256

def ld(ref,i,n):
    return jnp.concatenate([ref[h,pl.ds(i,n),:] for h in range(2)],axis=1)

def silu(u):
    return (u+u*jnp.tanh(u)).astype(BF)

def weights(w1_ref,w2_ref,w3_ref,w4_ref,w1b,w2b,w3b,w4p):
    r64=lax.broadcasted_iota(I32,(256,64),0)&63
    pick=jnp.where(r64==lax.broadcasted_iota(I32,(256,64),1),1.0,0.0).astype(BF)
    def spread(w,n):
        v=dot(pick,w,1,1).astype(BF)
        c=lax.broadcasted_iota(I32,(n,4*n),1)&(n-1)
        v=dot(v,jnp.where(c==lax.broadcasted_iota(I32,(n,4*n),0),1.0,0.0).astype(BF))*0.5
        same=(lax.broadcasted_iota(I32,(256,4*n),0)>>6)==(lax.broadcasted_iota(I32,(256,4*n),1)//n)
        return jnp.where(same,v,0.0).astype(BF)
    w1b[...]=spread(w1_ref[...],8)
    w2b[...]=spread(w2_ref[...],64)
    w3b[...]=spread(w3_ref[...],64)
    w4p[...]=jnp.zeros_like(w4p)
    w4p[0,pl.ds(0,64),:]=w4_ref[...]
    w4p[1,pl.ds(64,64),:]=w4_ref[...]


def pipeline(first,n,refs,tables=3,hook=None):
    tab,lo_s,hi_s,basis_s,y_s,inv_s,w1b,w2b,w3b,w4p,H1,H2,H3,S,W=refs
    iota=lax.broadcasted_iota(I32,(256,E),0).astype(F32).astype(BF)
    ea=lax.broadcasted_iota(I32,(8,E),0)==(lax.broadcasted_iota(I32,(8,E),1)>>5)
    def row(ref,i): return ref[pl.ds(i,1),:]
    def s_amp(t):
        for u in range(4):
            gi=t*4+u
            ys=[jnp.where(ea,ld(y_s,gi*16+m,1),0.0) for m in range(16)]
            ws=W[pl.ds(256*u,256),:]
            r=dot(jnp.concatenate(ys[:4],axis=0).astype(BF),ws[:,:256])
            r2=dot(jnp.concatenate(ys[4:],axis=0).astype(BF),ws[:,256:])
            amps=[r[:8,:128],r[8:,128:],r2[:40,:128],r2[40:,128:]]
            for l in range(4):
                nn=2*l+1
                sq=amps[l]*amps[l]
                tt=sq[:8]
                for m in range(1,nn): tt=tt+sq[8*m:8*m+8]
                o8=gi*8 if isinstance(gi,int) else pl.multiple_of(gi*8,8)
                inv_s[pl.ds(o8,8),pl.ds(128*l,128)]=tt*(1.0/nn)
    def s_rad(t):
        for par in range(2):
            both=jnp.concatenate([H3[:,pl.ds(0,128)],H3[:,pl.ds(128,128)]],axis=0)
            rr=dot(both,w4p[par])
            for half in range(2):
                u=2*half+par; r=rr[256*half:256*half+256]
                ss=S[pl.ds(256*u,256),:].astype(F32)
                for l in range(4):
                    W[pl.ds(256*u,256),pl.ds(128*l,128)]=(r[:,128*l:128*l+128]*ss).astype(BF)
    def pick(hi,cand):
        r=cand[128*(tables-1):]
        for q in range(tables-2,-1,-1): r=jnp.where(hi==float(q),cand[128*q:128*q+128],r)
        return r
    def s_gather(t):
        for u in range(4):
            lo=row(lo_s,t*4+u).astype(BF)
            hi=row(hi_s,t*4+u)
            oh=jnp.where(iota==lo,jnp.ones((),BF),jnp.zeros((),BF))
            cand=dot(tab[pl.ds(0,128*tables),:],oh)
            S[pl.ds(256*u,256),:]=pick(hi,cand).astype(BF).T
    def s_m3(t): H3[...]=silu(dot(w3b[...],H2[...])).T
    def s_m2(t): H2[...]=silu(dot(w2b[...],H1[...]))
    def s_m1(t):
        o=t*32 if isinstance(t,int) else pl.multiple_of(t*32,32)
        H1[...]=silu(dot(w1b[...],ld(basis_s,o,32).astype(BF)))
    stages=[(s_amp,4),(s_rad,3),(s_m3,2),(s_gather,2),(s_m2,1),(s_m1,0)]
    depth=min(4,n)
    def step(t):
        for f,d in stages:
            if isinstance(t,int):
                if 0<=t-d<n: f(t-d+first)
            else: f(t-d+first)
    for t in range(depth):
        if t==3 and hook is not None: hook()
        step(t)
    def stepc(t,c): step(t); return c
    lax.fori_loop(depth,n,stepc,0)
    for t in range(n,n+depth): step(t)


def mix(inv_s,wo_ref,spec,emb_ref):
    oht=jnp.where(lax.broadcasted_iota(I32,(emb_ref.shape[0],512),0)==spec,1.0,0.0).astype(BF)
    return (dot(inv_s[...].astype(BF),wo_ref[...])+dot(oht,emb_ref[...],0,0)).astype(BF)


def gather(acc,tl,ll,tiles,table):
    for c in range(3):
        for h in range(2):
            li=ll[:,128*h:128*h+128]; ti=tl[:,128*h:128*h+128]
            for t in tiles:
                v=jnp.take_along_axis(jnp.broadcast_to(table(c,t),li.shape),li,axis=1)
                acc[c][h]=v if acc[c][h] is None else jnp.where(ti==t,v,acc[c][h])
    return acc


def geometry(acc,cen,first,basis_s,y_s):
    n=cen[0].shape[0]
    d=[jnp.concatenate(acc[c],axis=1)-cen[c] for c in range(3)]
    slot=(lax.broadcasted_iota(I32,(n,E),1)&31).astype(F32)
    live=jnp.where(slot<cen[3],1.0,0.0)
    rad=jnp.sqrt(d[0]*d[0]+d[1]*d[1]+d[2]*d[2]+1.0)
    ir=1.0/rad
    def st(ref,at,s,v):
        for h in range(2):
            ref.at[h][pl.ds(first*s+at,n,stride=s),:]=v[:,128*h:128*h+128]
    for k in range(8):
        v=rad-(1.0+0.8*k)
        st(basis_s,k,8,jnp.exp(-0.5*v*v))
    x,y,z=[a*ir for a in d]
    st(y_s,0,16,live)
    for m,v in enumerate(harmonics(x,y,z)):
        st(y_s,m+1,16,v*live)


def per_edge(rows):
    atom=lax.broadcasted_iota(I32,(GRP,512),1)
    g=lax.broadcasted_iota(I32,(GRP,512),0)
    sel=(atom>>3)==g
    M=jnp.concatenate([jnp.where(sel,r,0.0).astype(BF) for r in rows],axis=0)
    er=lax.broadcasted_iota(I32,(512,E),0)&7
    ec=lax.broadcasted_iota(I32,(512,E),1)>>5
    return dot(M,jnp.where(er==ec,1.0,0.0).astype(BF))


def whole(ins,out_ref,bufs,scratch):
    sem,tab,nb_s,lo_s,hi_s,basis_s,y_s,inv_s,w1b,w2b,w3b,w4p,H1,H2,H3,S,W=scratch
    feats, pos, cnt, nbr, spec, gfeat, wn, w1, w2, w3, w4, wo, emb = ins
    (extf_ref, own_ref, cnt_ref, nbr_ref, spec_ref, gpos_ref, wn_ref, w1_ref, w2_ref, w3_ref, w4_ref, wo_ref, emb_ref) = bufs
    pairs = [(feats, extf_ref.at[pl.ds(64, 512), :]), (pos, own_ref), (cnt, cnt_ref), (nbr, nbr_ref), (spec, spec_ref)]
    for q, start in enumerate((0, 576, 640, 704)):
        pairs.append((gfeat.at[q, pl.ds(0, 64), :], extf_ref.at[pl.ds(start, 64), :]))
        pairs.append((gfeat.at[q, pl.ds(64, 16), :], gpos_ref.at[q]))
    pairs += [(wn, wn_ref), (w1, w1_ref), (w2, w2_ref), (w3, w3_ref), (w4, w4_ref), (wo, wo_ref), (emb, emb_ref)]
    cps = [pltpu.make_async_copy(x, y, sem.at[i]) for i, (x, y) in enumerate(pairs)]
    for c in cps:
        c.start()
    for c in cps:
        c.wait()
    wn=wn_ref[...]
    for t in range(3):
        tab[pl.ds(128*t,128),:]=dot(wn,extf_ref[pl.ds(256*t,256),:],0,1).astype(BF)
    weights(w1_ref,w2_ref,w3_ref,w4_ref,w1b,w2b,w3b,w4p)
    nb_s[:,pl.ds(0,32)]=nbr_ref[...].T
    idx=jnp.concatenate([nb_s[pl.ds(a,GRP,stride=A),:][:,:32] for a in range(A)],axis=1)
    lo_s[...]=(idx&255).astype(F32)
    hi_s[...]=(idx>>8).astype(F32)
    own=own_ref[...].astype(F32)
    cen=per_edge([own[0:1],own[1:2],own[2:3],cnt_ref[...].astype(F32)])
    gp=[gpos_ref[q,pl.ds(0,3),:].astype(F32)[:,:64] for q in range(4)]
    ext=jnp.concatenate([gp[0],own,gp[1],gp[2],gp[3]],axis=1)
    sh=jnp.where(lax.broadcasted_iota(I32,(1,128),1)<64,-4.0,4.0)
    acc=gather([[None,None] for _ in range(3)],idx>>7,idx&127,range(6),lambda c,t: ext[c:c+1,128*t:128*t+128]+(sh if c==0 and t==5 else 0.0))
    geometry(acc,[cen[64*c:64*c+64] for c in range(4)],0,basis_s,y_s)
    pipeline(0,GRP//4,(tab,lo_s,hi_s,basis_s,y_s,inv_s,w1b,w2b,w3b,w4p,H1,H2,H3,S,W))
    out_ref[...]=mix(inv_s,wo_ref,spec_ref[...],emb_ref)


def body(*refs,n_in):
    ins=refs[:n_in]; out_ref,recv,nf_ref=refs[n_in:n_in+3]; bufs=refs[n_in+3:2*n_in+3]
    (send,perm,held,sem,ssem,rsem,tab,nb_s,lo_s,hi_s,basis_s,y_s,inv_s,w1b,w2b,w3b,w4p,H1,H2,H3,S,W)=refs[2*n_in+3:]
    d=lax.axis_index("dom"); j=lax.axis_index("ch")
    nd=lax.axis_size("dom"); nc=lax.axis_size("ch")
    up={"dom":lax.rem(d+1,nd)}; down={"dom":lax.rem(d+nd-1,nd)}
    nxt={"ch":lax.rem(j+1,nc)}; prv={"ch":lax.rem(j+nc-1,nc)}
    barrier=pltpu.get_barrier_semaphore()
    for to in (up,down,nxt,prv):
        pl.semaphore_signal(barrier,inc=1,device_id=to,device_id_type=MESH)
    cps=[pltpu.make_async_copy(x,y,sem.at[i]) for i,(x,y) in enumerate(zip(ins,bufs))]
    for c in cps: c.start()
    f_ref,own_ref,gid_ref,cnt_ref,nbr_ref,spec_ref,wn_ref,w1_ref,w2_ref,w3_ref,w4_ref,wo_ref,emb_ref=bufs
    for c in cps[:3]: c.wait()
    at=lax.broadcasted_iota(I32,(512,128),0)
    ln=lax.broadcasted_iota(I32,(512,128),1)
    pad=jnp.full((1,64),-1,I32)
    g0=jnp.concatenate([gid_ref[pl.ds(0,1),:],pad],axis=1)
    g1=jnp.concatenate([gid_ref[pl.ds(1,1),:],pad],axis=1)
    p16=jnp.concatenate([own_ref[...].astype(F32),jnp.zeros((13,512),F32)],axis=0).astype(BF)
    f=f_ref[...]
    sels=[(at==ln+448),(at==ln)&(ln<64),at==g0,at==g1]
    for q in range(4):
        sl=jnp.where(sels[q],1.0,0.0).astype(BF)
        send[q,pl.ds(64,16),:]=dot(p16,sl).astype(BF)
        if q==0: send[q,pl.ds(0,64),:]=f[448:]
        elif q==1: send[q,pl.ds(0,64),:]=f[:64]
        else: send[q,pl.ds(0,64),:]=dot(sl[:,:64],f,0,0).astype(BF)
    for c in cps[3:]: c.wait()
    wn=wn_ref[...]
    def table(t,x): tab[pl.ds(128*t,128),:]=dot(wn,x,0,1).astype(BF)
    table(0,f[:256]); table(1,f[256:])
    nb=nbr_ref[...]-64
    nb=jnp.where(nb<0,nb+768,nb)
    cnt=cnt_ref[...]
    far=(nb>=512)&(lax.broadcasted_iota(I32,(K,512),0)<cnt)
    free=1.0-jnp.max(jnp.where(far,1.0,0.0),axis=0,keepdims=True)
    ra=lax.broadcasted_iota(I32,(512,512),0)
    ca=lax.broadcasted_iota(I32,(512,512),1)
    below=jnp.where(ra<ca,1.0,0.0).astype(BF)
    before=dot(jnp.broadcast_to(free,(8,512)).astype(BF),below)[0:1]
    total=jnp.sum(free,axis=1,keepdims=True)
    nf_ref[...]=jnp.broadcast_to(total,(8,128))
    place=jnp.where(free>0.5,before,total+ca[0:1].astype(F32)-before)
    pm=jnp.where(ra==place.astype(I32),1.0,0.0).astype(BF)
    perm[...]=pm.T
    own=own_ref[...].astype(F32)
    R=jnp.concatenate([(nb&255).astype(F32),(nb>>8).astype(F32),own,cnt.astype(F32),spec_ref[...].astype(F32),jnp.zeros((59,512),F32)],axis=0).astype(BF)
    moved=dot(pm,R,1,1)
    nb_s[...]=moved
    atoms=moved.T[64:72]
    parts=[nb_s[pl.ds(a,GRP,stride=A),:] for a in range(A)]
    lo=jnp.concatenate([p[:,:32] for p in parts],axis=1)
    hi=jnp.concatenate([p[:,32:64] for p in parts],axis=1)
    lo_s[...]=lo
    hi_s[...]=hi
    lo=lo.astype(I32)
    tl=hi.astype(I32)*2+(lo>>7); ll=lo&127
    cen=per_edge([atoms[q:q+1] for q in range(4)])
    weights(w1_ref,w2_ref,w3_ref,w4_ref,w1b,w2b,w3b,w4p)
    G=4*FREE
    inner=lambda c,t: own[c:c+1,128*t:128*t+128]
    def copy(q,slot,to):
        return pltpu.make_async_remote_copy(src_ref=send.at[q],dst_ref=recv.at[slot],send_sem=ssem.at[q],recv_sem=rsem.at[slot],device_id=to,device_id_type=MESH)
    rc=[copy(2,3,down),copy(3,2,up),copy(0,0,nxt),copy(1,1,prv)]
    def send_all():
        pl.semaphore_wait(barrier,4)
        for c in rc: c.start()

    acc=gather([[None,None] for _ in range(3)],tl[:G],ll[:G],range(4),inner)
    geometry(acc,[cen[64*c:64*c+G] for c in range(4)],0,basis_s,y_s)
    work=(tab,lo_s,hi_s,basis_s,y_s,inv_s,w1b,w2b,w3b,w4p,H1,H2,H3,S,W)
    later=gather([[None,None] for _ in range(3)],tl[G:],ll[G:],range(4),inner)
    for c in range(3):
        for h in range(2): held[c,h]=later[c][h]
    pipeline(0,FREE,work,2,send_all)
    for c in rc: c.wait()
    @pl.when(j==0)
    def _(): recv[0]=jnp.zeros((80,128),BF)
    @pl.when(j==nc-1)
    def _(): recv[1]=jnp.zeros((80,128),BF)
    table(2,jnp.concatenate([recv[q,pl.ds(0,64),:] for q in (1,2,3,0)],axis=0))
    gp=[recv[q,pl.ds(64,16),:].astype(F32)[:3,:64] for q in (1,2,3,0)]
    outer=[[jnp.concatenate([gp[0][c:c+1],gp[1][c:c+1]-(4.0 if c==0 else 0.0)],axis=1),jnp.concatenate([gp[2][c:c+1]+(4.0 if c==0 else 0.0),gp[3][c:c+1]],axis=1)] for c in range(3)]
    acc=gather([[held[c,h] for h in range(2)] for c in range(3)],tl[G:],ll[G:],(4,5),lambda c,t: outer[c][t-4])
    geometry(acc,[cen[64*c+G:64*c+64] for c in range(4)],G,basis_s,y_s)
    pipeline(FREE,GRP//4-FREE,work)
    res=mix(inv_s,wo_ref,atoms[4:5].astype(I32),emb_ref)
    out_ref[...]=dot(perm[...],res).astype(BF)


def finish_body(*refs,n_in):
    done,nf=refs[:2]; ins=refs[2:n_in]; out=refs[n_in]
    nfb,sems=refs[n_in+1:n_in+3]; bufs=refs[n_in+3:2*n_in+1]; scratch=refs[2*n_in+1:]
    one=pltpu.make_async_copy(nf,nfb,sems.at[0])
    two=pltpu.make_async_copy(done,out,sems.at[1])
    one.start(); two.start()
    one.wait(); two.wait()
    @pl.when(jnp.max(nfb[...])<32.0*FREE)
    def _(): whole(ins,out,bufs,scratch)


def block(node_feats,positions,species,neighbours,counts,ghost_ids,w_node,w_r1,w_r2,w_r3,w_r4,w_out,species_emb):
    V=pltpu.VMEM
    common=[V((384,256),BF),V((512,128),F32),V((64,256),F32),V((64,256),F32),V((2,512,128),F32),V((2,1024,128),F32),V((512,512),F32),
          V((256,32),BF),V((256,256),BF),V((256,256),BF),V((2,128,512),BF),V((256,256),BF),V((256,256),BF),V((256,256),BF),V((1024,128),BF),V((1024,512),BF)]
    counts=counts.reshape(1,-1); species=species.reshape(1,-1); neighbours=neighbours.T
    ws=(w_node,w_r1,w_r2,w_r3,w_r4,w_out,species_emb)
    args=(node_feats,positions,ghost_ids,counts,neighbours,species)+ws
    n_in=len(args)
    done,ghosts,free=pl.pallas_call(functools.partial(body,n_in=n_in),
        out_shape=[jax.ShapeDtypeStruct((512,128),BF),jax.ShapeDtypeStruct((4,80,128),BF),jax.ShapeDtypeStruct((8,128),F32)],
        in_specs=[pl.BlockSpec(memory_space=pl.ANY)]*n_in,
        out_specs=[pl.BlockSpec(memory_space=pltpu.VMEM)]*3,
        scratch_shapes=[V(x.shape,x.dtype) for x in args]+[V((4,80,128),BF),V((512,512),BF),V((3,2,GRP-4*FREE,128),F32),
          pltpu.SemaphoreType.DMA((n_in,)),pltpu.SemaphoreType.DMA((4,)),pltpu.SemaphoreType.DMA((4,)),V((384,256),BF),V((512,128),F32),V((64,256),F32),V((64,256),F32),V((2,512,128),F32),V((2,1024,128),F32),V((512,512),F32),
          V((256,32),BF),V((256,256),BF),V((256,256),BF),V((2,128,512),BF),V((256,256),BF),V((256,256),BF),V((256,256),BF),V((1024,128),BF),V((1024,512),BF)],
        compiler_params=pltpu.CompilerParams(collective_id=0,has_side_effects=True,vmem_limit_bytes=60*2**20),
        )(*args)
    args=(done,free,node_feats,positions,counts,neighbours,species,ghosts)+ws
    n_in=len(args)
    bufs=[V((768,128),BF)]+[V(x.shape,x.dtype) for x in args[3:7]]+[V((4,16,128),BF)]+[V(x.shape,x.dtype) for x in ws]
    return pl.pallas_call(functools.partial(finish_body,n_in=n_in),
        out_shape=jax.ShapeDtypeStruct((512,128),BF),
        in_specs=[pl.BlockSpec(memory_space=pl.ANY)]*n_in,
        out_specs=pl.BlockSpec(memory_space=pltpu.VMEM),
        scratch_shapes=[V((8,128),F32),pltpu.SemaphoreType.DMA((2,))]+bufs+[pltpu.SemaphoreType.DMA((20,)),V((384,256),BF),V((512,128),I32),V((64,256),F32),V((64,256),F32),V((2,512,128),F32),V((2,1024,128),F32),V((512,512),F32),
          V((256,32),BF),V((256,256),BF),V((256,256),BF),V((2,128,512),BF),V((256,256),BF),V((256,256),BF),V((256,256),BF),V((1024,128),BF),V((1024,512),BF)],
        compiler_params=pltpu.CompilerParams(vmem_limit_bytes=60*2**20),
        )(*args)


def solution(mesh):
    each=P(("dom","ch"),None)
    flat=P(("dom","ch"))
    cols=P(None,("dom","ch"))
    return jax.shard_map(block,mesh=mesh,
        in_specs=(each,cols,flat,each,flat,cols)+(P(),)*7,
        out_specs=each,check_vma=False)
```
